128 devices in a mesh: replica: 32 (over x, z, y_hi), fsdp: 4 (over y_lo, core).
Axes of the slice: x: 4, y: 4 (y_hi: 2, y_lo: 2; y = y_hi * 2 + y_lo), z: 4, core: 2. Of those that a mesh axis runs over, the one named last changes fastest.
Arguments:
- hidden_act: bfloat16 [131072, 512], P(('replica', 'fsdp')), may hold values from -6 to 6
- out_grad: bfloat16 [131072, 5120], P(('replica', 'fsdp')), may hold values from -6 to 6
- momentum: float32 [32, 512, 5120], P('replica', 'fsdp'), may hold values from -6 to 6
- coef_picks: int32 [32, 8, 80, 32], P('replica', 'fsdp'), may hold values from 0 to 63, as said below
- params: bfloat16 [512, 5120], P('fsdp'), may hold values from -6 to 6
Outputs:
- momentum_left: float32 [32, 512, 5120], P('replica', 'fsdp')
- update: float32 [512, 5120], P('fsdp')
- new_params: bfloat16 [512, 5120], replicated
The draws below stay inside these ranges and needn't reach their ends.
Inputs may be any that keep to these rules, and one draw needn't show every extreme that they name: `coef_picks`: for every replica and span, the first 16 entries are distinct, and so are the last 16.
All inputs are finite; a program needn't handle non-finite values.
Results may differ from the reference program's by a relative error of at most 0.001.
Values may be sent and summed in bfloat16 or wider, within the bound.
No kernel may reach another device: no remote copies, remote signals or barrier semaphores. Data moves between devices by JAX's collectives and lax.ppermute only.
A program may use at most 256 MiB of HBM per device.

```python
import math
import jax
import jax.numpy as jnp
from jax import lax

D = 5120
ROWS = 512
KEEP = 16
TOK_DEV = 1024
TOKENS = 131072
N_REPLICA = 32
N_FSDP = 4


def draw_coef_picks(key, part):
    key = jax.random.fold_in(key, 7)
    grid_shape = (N_REPLICA, ROWS // 64, D // 64, 2, 64)
    scores = jax.random.randint(key, grid_shape, 0, 2 ** 20) * 64 + jnp.arange(64, dtype=jnp.int32)
    ranked = jnp.argsort(scores, axis=-1)[..., :KEEP]
    return ranked.reshape(N_REPLICA, ROWS // 64, D // 64, 2 * KEEP).astype(jnp.int32)


def shard_levels(rng, dims, split, least, largest):
    def one(dim, parts):
        steps = jax.random.uniform(jax.random.fold_in(jax.random.fold_in(rng, 6), dim), (parts,), jnp.float32, least / len(split), largest / len(split))
        return jnp.repeat(jnp.exp(steps), dims[dim] // parts).reshape((-1,) + (1,) * (len(dims) - dim - 1))

    loudness = one(*split[0])
    for cut in split[1:]:
        loudness = loudness * one(*cut)
    return loudness


def gaussian(own_key, extent, width, bound, shards=(), held_as=jnp.bfloat16):
    array = width * jax.random.normal(own_key, extent, jnp.float32)
    if shards:
        array = array * shard_levels(own_key, extent, shards, -0.22, 0.18)
    return jnp.clip(array, -bound, bound).astype(held_as)


def setup_inputs(seed: int = 0) -> dict:
    arg_keys = jax.random.split(jax.random.key(seed), 6)
    return {
        "hidden_act": gaussian(arg_keys[0], (TOKENS, ROWS), 1.0, 6.0, ((0, 128),)),
        "out_grad": gaussian(arg_keys[1], (TOKENS, D), 1.0, 6.0, ((0, 128),)),
        "momentum": gaussian(arg_keys[2], (N_REPLICA, ROWS, D), 1.0, 6.0, ((0, 32), (1, 4)), jnp.float32),
        "coef_picks": draw_coef_picks(jax.random.fold_in(arg_keys[5], 71), 0),
        "params": gaussian(arg_keys[4], (ROWS, D), 1.0, 6.0, ((0, 4),)),
    }


momentum_decay = 0.9
step_size = 0.5

def cosine_table():
    freq_index = jnp.arange(64, dtype=jnp.float32)[:, None]
    place_index = jnp.arange(64, dtype=jnp.float32)[None, :]
    row_weight = jnp.where(freq_index == 0, math.sqrt(1.0 / 64), math.sqrt(2.0 / 64))
    return row_weight * jnp.cos(math.pi * (2.0 * place_index + 1.0) * freq_index / 128.0)

def select_hot(chosen):
    return (chosen[..., None] == jnp.arange(64, dtype=jnp.int32)).astype(jnp.float32)

def compress_spans(moment, chosen, table_dct):
    span_rows = moment.shape[0] // 64
    span_cols = moment.shape[1] // 64
    blocks = moment.reshape(span_rows, 64, span_cols, 64)
    row_hot = select_hot(chosen[..., :KEEP])
    col_hot = select_hot(chosen[..., KEEP:])
    row_basis = jnp.einsum('abuk,kj->abuj', row_hot, table_dct, precision=lax.Precision.HIGHEST)
    col_basis = jnp.einsum('abuk,kj->abuj', col_hot, table_dct, precision=lax.Precision.HIGHEST)
    coeffs = jnp.einsum('abui,aibj,abvj->abuv', row_basis, blocks, col_basis, precision=lax.Precision.HIGHEST)
    removed = jnp.einsum('abui,abuv,abvj->aibj', row_basis, coeffs, col_basis, precision=lax.Precision.HIGHEST)
    placed = jnp.einsum('abui,abuv,abvj->abij', row_hot, coeffs, col_hot, precision=lax.Precision.HIGHEST)
    return (coeffs, removed.reshape(moment.shape), placed)

def reference(hidden_act, out_grad, momentum, coef_picks, params):
    per_replica = TOK_DEV * N_FSDP
    table_dct = cosine_table()
    grad_scale = 1.0 / math.sqrt(per_replica)
    acts_split = hidden_act.reshape(N_REPLICA, per_replica, ROWS)
    grads_split = out_grad.reshape(N_REPLICA, per_replica, D)

    def replica_step(grid_sum, inputs):
        act_rows, grad_rows, moment_old, chosen = inputs
        gradient = jnp.dot(act_rows.T, grad_rows, preferred_element_type=jnp.float32) * grad_scale
        moment_new = momentum_decay * moment_old + gradient
        coeffs, removed, placed = compress_spans(moment_new, chosen, table_dct)
        return (grid_sum + placed, moment_new - removed)
    zero_grid = jnp.zeros((ROWS // 64, D // 64, 64, 64), jnp.float32)
    grid, momentum_left = lax.scan(replica_step, zero_grid, (acts_split, grads_split, momentum, coef_picks))
    update = jnp.einsum('pi,abpq,qj->aibj', table_dct, grid, table_dct, precision=lax.Precision.HIGHEST).reshape(ROWS, D)
    new_params = (params.astype(jnp.float32) - step_size * update).astype(jnp.bfloat16)
    return (momentum_left, update, new_params)
```

```python
import functools
import math

import jax
import jax.numpy as jnp
import numpy as np
from jax import lax
from jax.experimental import pallas as pl
from jax.experimental.pallas import tpu as pltpu
from jax.sharding import Mesh
from jax.sharding import PartitionSpec as P

KEEP = 16
DECAY = 0.9
STEP = 0.5
PARTS = 2
PAIRS = 8
PER = PAIRS // PARTS
GW = 640
QROWS = 656
UROWS = 176
F32 = jnp.float32
BF16 = jnp.bfloat16
I16 = jnp.int16
I32 = jnp.int32
ARB = pltpu.CompilerParams(vmem_limit_bytes=48 * 1024 * 1024)


def cosine():
    k = np.arange(64, dtype=np.float64)[:, None]
    i = np.arange(64, dtype=np.float64)[None, :]
    w = np.where(k == 0, math.sqrt(1.0 / 64), math.sqrt(2.0 / 64))
    return w * np.cos(math.pi * (2.0 * i + 1.0) * k / 128.0)


def halves(m):
    hi = m.astype(np.float32).astype(jnp.bfloat16)
    lo = (m - hi.astype(np.float64)).astype(np.float32).astype(jnp.bfloat16)
    return hi, lo


def diag(m, n):
    return np.kron(np.eye(n), m)


def right_table(m):
    hi, lo = halves(m)
    row = np.concatenate([hi, lo], axis=1)
    return np.concatenate([row, row], axis=0)


def left_table(m):
    return np.concatenate(halves(m), axis=0)


def split(x):
    hi = x.astype(BF16)
    return hi, (x - hi.astype(F32)).astype(BF16)


def mul_right(x, table):
    hi, lo = split(x)
    o = jnp.dot(jnp.concatenate([hi, lo], axis=1), table, preferred_element_type=F32)
    return o[:, :128] + o[:, 128:]


def mul_left(table, x):
    n = table.shape[0] // 2
    hi, lo = split(x)
    o = jnp.dot(table, hi, preferred_element_type=F32)
    return o[:n] + o[n:] + jnp.dot(table[:n], lo, preferred_element_type=F32)


def lanes_of(x, idx):
    return jnp.take_along_axis(x, jnp.broadcast_to(idx, x.shape), axis=1, mode="promise_in_bounds")


def rows_of(x, idx):
    return jnp.take_along_axis(x, idx, axis=0, mode="promise_in_bounds")


def lane(shape):
    return lax.broadcasted_iota(I32, shape, len(shape) - 1)


def sub(shape):
    return lax.broadcasted_iota(I32, shape, 0)


def pow2(e):
    n = e + 100
    r = jnp.full(e.shape, 2.0**-100, F32)
    for bit in range(7):
        r = r * jnp.where((n >> bit) & 1 == 1, 2.0 ** (1 << bit), 1.0)
    r = r * jnp.where((n >> 7) & 1 == 1, 2.0**64, 1.0)
    return r * jnp.where((n >> 7) & 1 == 1, 2.0**64, 1.0)


def exponent(top):
    e = jnp.floor(math.log2(32767.0) - jnp.log(jnp.maximum(top, 1e-35)) * (1 / math.log(2)))
    return jnp.clip(e, -60.0, 99.0).astype(I32)


def coded(x, e):
    v = jnp.floor(x * pow2(e) + 0.5)
    return jnp.clip(v, -32767.0, 32767.0).astype(I32).astype(I16)


def value(q, e):
    return q.astype(I32).astype(F32) * pow2(-e)


def gradient_kernel(me, h_ref, g_ref, own_ref, other_ref, ht):
    @pl.when(pl.program_id(0) == 0)
    def _():
        yl, core = me[0], me[1]
        for i, (y, c) in enumerate(((yl, core), (1 - yl, core), (yl, 1 - core), (1 - yl, 1 - core))):
            at = pl.multiple_of(128 * (2 * y + c), 128)
            ht[128 * i : 128 * i + 128, :] = h_ref[:, pl.ds(at, 128)].T

    other_ref[...] = jnp.dot(ht[256:], g_ref[...], preferred_element_type=F32)
    own_ref[...] = jnp.dot(ht[:256], g_ref[...], preferred_element_type=F32)


def gradient(me, hidden, grad, part):
    cols = 5120 // PARTS
    tile = 512
    n = cols // tile
    spec = pl.BlockSpec((256, tile), lambda i, me: (0, i))
    return pl.pallas_call(
        gradient_kernel,
        grid_spec=pltpu.PrefetchScalarGridSpec(
            num_scalar_prefetch=1,
            grid=(n,),
            in_specs=[
                pl.BlockSpec((1024, 512), lambda i, me: (0, 0)),
                pl.BlockSpec((1024, tile), lambda i, me: (0, part * n + i)),
            ],
            out_specs=[spec, spec],
            scratch_shapes=[pltpu.VMEM((512, 1024), BF16)],
        ),
        out_shape=[jax.ShapeDtypeStruct((256, cols), F32)] * 2,
        compiler_params=ARB,
        cost_estimate=pl.CostEstimate(flops=2 * 512 * 1024 * cols, bytes_accessed=8 * 2**20, transcendentals=0),
        name="gradient",
    )(me, hidden, grad)


def place(group, pos):
    return pos if group == 0 else 5 + (pos + 1) % 5


def pick_tables():
    t = np.zeros((2, 8, 128), np.int32)
    for g in range(2):
        for ln in range(128):
            pos = min(ln // 16, 4) if ln < 80 else (ln - 80 if ln < 85 else 0)
            t[g, 0, ln] = place(g, pos)
            t[g, 1, ln] = 64 * (place(g, pos) % 2) if ln < 80 else 0
            for tile in range(3):
                t[g, 2 + tile, ln] = place(g, min(2 * tile + ln // 64, 4))
    return t


def compress_kernel(part, me, own, got, mom, picks, tab, rt, lt, *refs):
    pm, q, comp = refs[-3:]
    yl = me[0]
    first = 10 * (PER * part + pl.program_id(0))
    ln = lane((1, 128))
    w0 = (own[:128] + got[:128]) * (1.0 / 64) + DECAY * mom[0]
    w1 = (own[128:] + got[128:]) * (1.0 / 64)
    pm[...] = w0
    exps = jnp.zeros((16, 128), I32)
    tiles = []
    for t in range(5):
        x = w1[:, 128 * t : 128 * t + 128]
        e = exponent(jnp.max(jnp.abs(x), axis=0, keepdims=True))
        q[0, 128 * t : 128 * t + 128, :] = coded(x, jnp.broadcast_to(e, (8, 128))[:1])
        exps = jnp.where(sub((16, 128)) == t, jnp.broadcast_to(e, (16, 128)), exps)
        tiles.append(mul_right(jnp.concatenate([w0[:, 128 * t : 128 * t + 128], x], axis=0), rt[...]))
    q[0, 640:656, :] = exps.astype(I16)
    u16 = sub((16, 128))
    ln16 = lane((16, 128))
    short = []
    for g in range(2):
        pieces = []
        span = first + tab[g, 0:1, :]
        for rb in range(4):
            qt = picks[rb // 2, rb % 2, 16:32, :]
            chosen = jnp.where(u16 == (ln16 & 15), lanes_of(qt, span), 0)
            idx = jnp.sum(chosen, axis=0, keepdims=True) + tab[g, 1:2, :]
            rows = slice(64 * rb, 64 * rb + 64)
            a = lanes_of(tiles[3 * g][rows], idx)
            b = lanes_of(tiles[3 * g + 1][rows], idx)
            c = lanes_of(tiles[2][rows], idx)
            pieces.append(jnp.where(ln < 32, a, jnp.where(ln < 64, b, c)))
        short.append(jnp.concatenate(pieces, axis=0))
    z = mul_left(lt[...], jnp.concatenate(short, axis=1))
    for g in range(2):
        span = first + tab[g, 0:1, :]
        for rb in range(4):
            rel, a = rb // 2, rb % 2
            to = yl if rel == 0 else 1 - yl
            pt = picks[rel, a, 0:16, :]
            qt = picks[rel, a, 16:32, :]
            pidx = lanes_of(pt, span)
            for h in range(2):
                pi = pidx[8 * h : 8 * h + 8]
                low, high = pi & 7, pi >> 3
                acc = pi.astype(F32)
                for j in range(8):
                    r = 64 * rb + 8 * j
                    v = rows_of(z[r : r + 8, 128 * g : 128 * g + 128], low)
                    acc = jnp.where((high == j) & (ln < 80), v, acc)
                comp[a, g, to, 8 * h : 8 * h + 8, :] = acc
            back = jnp.full((8, 128), -1, I32)
            for t in range(3):
                qg = lanes_of(qt, first + tab[g, 2 + t : 3 + t, :])
                src = 16 * (2 * t + (ln16 >> 6)) + u16 + 1
                hit = jnp.where(qg == (ln16 & 63), src, 0)
                if t == 2:
                    hit = jnp.where(ln16 < 64, hit, 0)
                inv = jnp.sum(hit, axis=0, keepdims=True) - 1
                back = jnp.where(sub((8, 128)) == t, jnp.broadcast_to(inv, (8, 128)), back)
            comp[a, g, to, 16:24, :] = back.astype(F32)


def compress(part, me, own, got, mom, picks, tab, rt, lt, before):
    n = PER
    full = lambda *s: pl.BlockSpec(s, lambda i, me: (0,) * len(s))
    col = lambda r: pl.BlockSpec((r, GW), lambda i, me: (0, i))
    args = [own, got, mom, picks, tab, rt, lt]
    in_specs = [
        col(256),
        col(256),
        pl.BlockSpec((1, 128, GW), lambda i, me: (0, 0, part * n + i)),
        full(2, 2, 32, 128),
        full(2, 8, 128),
        full(256, 256),
        full(512, 256),
    ]
    alias = {}
    if before is not None:
        args.append(before)
        in_specs.append(pl.BlockSpec(memory_space=pl.ANY))
        alias = {8: 2}
    return pl.pallas_call(
        functools.partial(compress_kernel, part),
        grid_spec=pltpu.PrefetchScalarGridSpec(
            num_scalar_prefetch=1,
            grid=(n,),
            in_specs=in_specs,
            out_specs=[
                col(128),
                pl.BlockSpec((1, QROWS, 128), lambda i, me: (i, 0, 0)),
                pl.BlockSpec((2, 2, 2, 24, 128), lambda i, me: (0, part * n + i, 0, 0, 0)),
            ],
        ),
        out_shape=[
            jax.ShapeDtypeStruct((128, 5120 // PARTS), F32),
            jax.ShapeDtypeStruct((n, QROWS, 128), I16),
            jax.ShapeDtypeStruct((2, 16, 2, 24, 128), F32),
        ],
        input_output_aliases=alias,
        compiler_params=ARB,
        cost_estimate=pl.CostEstimate(flops=2 * 10**9, bytes_accessed=9 * 2**20, transcendentals=0),
        name="compress",
    )(me, *args)


def owner_kernel(got, rt, lt, out, xh, xl, hot):
    ln16 = lane((16, 128))

    def one(n, _):
        at = pl.multiple_of(16 * n, 16)
        x = got[n, 0:16, :]
        for t in range(3):
            idx = got[n, 16 + t : 17 + t, :].astype(I32)
            v = jnp.where(idx >= 0, lanes_of(x, jnp.maximum(idx, 0)), 0.0)
            hi, lo = split(v)
            xh[t, pl.ds(at, 16), :] = hi
            xl[t, pl.ds(at, 16), :] = lo
            p = lanes_of(x, 80 + 2 * t + (ln16 >> 6))
            hot[t, pl.ds(at, 16), :] = jnp.where(p == (ln16 & 63).astype(F32), 1.0, 0.0).astype(BF16)
        return 0

    lax.fori_loop(0, got.shape[0], one, 0, unroll=4)
    same = (sub((128, 128)) >> 6) == (lane((128, 128)) >> 6)
    tiles = []
    for t in range(3):
        dims = (((0,), (0,)), ((), ()))
        d = lax.dot_general(hot[t], xh[t], dims, preferred_element_type=F32)
        d = d + lax.dot_general(hot[t], xl[t], dims, preferred_element_type=F32)
        d = jnp.where(same, d, 0.0)
        u = mul_left(lt[...], mul_right(d, rt[...]))
        tiles.append(u[:64] + u[64:])
    last = tiles[2]
    ln = lane((32, 128))
    tiles[2] = jnp.where(ln < 64, last[:32], jnp.roll(last[32:], 64, axis=1))
    x = jnp.concatenate(tiles, axis=0)
    e = exponent(jnp.max(jnp.abs(x), axis=0, keepdims=True))
    out[0:160, :] = coded(x, e)
    out[160:176, :] = jnp.broadcast_to(e, (16, 128)).astype(I16)


def owner(got, rt, lt):
    return pl.pallas_call(
        owner_kernel,
        out_shape=jax.ShapeDtypeStruct((UROWS, 128), I16),
        scratch_shapes=[pltpu.VMEM((3, 1024, 128), BF16)] * 3,
        compiler_params=ARB,
        name="owner",
    )(got, rt, lt)


def decode(ref, a, y):
    group = []
    for g in range(2):
        e = ref[a, g, y, 160:176, :].astype(I32)[:1]
        group.append(value(ref[a, g, y, 0:160, :], e))
    even, odd = group
    lo = lane((32, 128)) < 64
    e2, o2 = even[128:160], odd[128:160]
    top = jnp.where(lo, e2, jnp.roll(o2, 64, axis=1))
    bottom = jnp.where(lo, jnp.roll(e2, 64, axis=1), o2)
    return [even[:64], even[64:128], jnp.concatenate([top, bottom], axis=0), odd[:64], odd[64:128]]


def finish_kernel(with_update, me, got, mine, theirs, *refs):
    yl = me[0]
    new = refs[-1]
    for rel in range(2):
        y = yl if rel == 0 else 1 - yl
        par = mine if rel == 0 else theirs
        for a in range(2):
            rows = slice(64 * a, 64 * a + 64)
            for t, u in enumerate(decode(got, a, y)):
                cols = slice(128 * t, 128 * t + 128)
                if with_update and rel == 0:
                    refs[-2][rows, cols] = u
                new[y, 0, rows, cols] = (par[rows, cols].astype(F32) - STEP * u).astype(BF16)


def finish(with_update, me, got, mine, theirs, before):
    col = pl.BlockSpec((128, GW), lambda i, me: (0, i))
    which = (lambda me: me[1]) if with_update else (lambda me: 1 - me[1])
    args = [got, mine, theirs]
    in_specs = [pl.BlockSpec((2, 2, 2, UROWS, 128), lambda i, me: (0, i, 0, 0, 0)), col, col]
    out_specs = [pl.BlockSpec((2, 1, 128, GW), lambda i, me: (0, which(me), 0, i))]
    out_shape = [jax.ShapeDtypeStruct((2, 2, 128, 5120), BF16)]
    alias = {}
    if with_update:
        out_specs.insert(0, col)
        out_shape.insert(0, jax.ShapeDtypeStruct((128, 5120), F32))
    else:
        args.append(before)
        in_specs.append(pl.BlockSpec(memory_space=pl.ANY))
        alias = {4: 0}
    return pl.pallas_call(
        functools.partial(finish_kernel, with_update),
        grid_spec=pltpu.PrefetchScalarGridSpec(
            num_scalar_prefetch=1, grid=(PAIRS,), in_specs=in_specs, out_specs=out_specs
        ),
        out_shape=out_shape,
        input_output_aliases=alias,
        compiler_params=ARB,
        name="finish",
    )(me, *args)


def left_kernel(part, q, pm, picks, rt, lt, irt, ilt, *refs):
    out, mask = refs[-2:]
    first = 10 * (PER * part + pl.program_id(0))

    @pl.when(pl.program_id(0) == 0)
    def _():
        for a in range(2):
            k = sub((64, 128))
            hit = jnp.zeros((64, 128), F32)
            for u in range(16):
                hit = jnp.where(picks[0, a, u : u + 1, :] == k, 1.0, hit)
            mask[64 * a : 64 * a + 64, :] = hit

    ln16 = lane((16, 128))
    for t in range(5):
        cols = slice(128 * t, 128 * t + 128)
        e = q[0, 640:656, :].astype(I32)[t : t + 1]
        m = pm[:, cols] + value(q[0, 128 * t : 128 * t + 128, :], e)
        c = mul_left(lt[...], mul_right(m, rt[...]))
        span = first + 2 * t + (lane((1, 128)) >> 6)
        keep = lanes_of(mask[...], span)
        parts = []
        for a in range(2):
            hit = lanes_of(picks[0, a, 16:32, :], span) == (ln16 & 63)
            parts.append(jnp.max(jnp.where(hit, 1.0, 0.0), axis=0, keepdims=True))
        rows = sub((128, 128)) < 64
        keep = keep * jnp.where(rows, parts[0], parts[1])
        r = mul_left(ilt[...], mul_right(c * keep, irt[...]))
        out[0, :, cols] = m - r


def left(part, q, pm, picks, rt, lt, irt, ilt, before):
    n = PER
    full = lambda *s: pl.BlockSpec(s, lambda i: (0,) * len(s))
    args = [q, pm, picks, rt, lt, irt, ilt]
    in_specs = [
        pl.BlockSpec((1, QROWS, 128), lambda i: (i, 0, 0)),
        pl.BlockSpec((128, GW), lambda i: (0, i)),
        full(2, 2, 32, 128),
        full(256, 256),
        full(256, 128),
        full(256, 256),
        full(256, 128),
    ]
    alias = {}
    if before is not None:
        args.append(before)
        in_specs.append(pl.BlockSpec(memory_space=pl.ANY))
        alias = {7: 0}
    return pl.pallas_call(
        functools.partial(left_kernel, part),
        grid=(n,),
        in_specs=in_specs,
        out_specs=pl.BlockSpec((1, 128, GW), lambda i: (0, 0, part * n + i)),
        out_shape=jax.ShapeDtypeStruct((1, 128, 5120), F32),
        scratch_shapes=[pltpu.VMEM((128, 128), F32)],
        input_output_aliases=alias,
        compiler_params=ARB,
        cost_estimate=pl.CostEstimate(flops=2 * 10**9, bytes_accessed=4 * 2**20, transcendentals=0),
        name="left",
    )(*args)


REP = ("x", "z", "yh", "yl")
NEAR = [(2 * h + k, 2 * h + 1 - k) for h in range(2) for k in range(2)]
FAR = [(y, 3 - y) for y in range(4)]
SWAP = [(0, 1), (1, 0)]


def body(hidden, grad, momentum, coef_picks, params):
    c = cosine()
    rt = jnp.asarray(right_table(diag(c.T, 2)))
    irt = jnp.asarray(right_table(diag(c, 2)))
    lt4 = jnp.asarray(left_table(diag(c, 4)))
    lt = jnp.asarray(left_table(diag(c, 2)))
    ilt = jnp.asarray(left_table(diag(c.T, 2)))
    tab = jnp.asarray(pick_tables())
    me = jnp.stack([lax.axis_index("yl"), lax.axis_index("c")]).astype(I32)

    mine = jnp.pad(coef_picks[0].swapaxes(1, 2), ((0, 0), (0, 0), (0, 48)))
    theirs = lax.ppermute(mine, ("yh", "yl"), NEAR)
    picks = jnp.stack([mine, theirs])
    far_params = lax.ppermute(params, ("yh", "yl"), FAR)

    pms, qs, comp = [], [], None
    grads = [gradient(me, hidden, grad, part) for part in range(PARTS)]
    swapped = [lax.ppermute(other, "c", SWAP) for _, other in grads]
    for part in range(PARTS):
        pm, q, comp = compress(part, me, grads[part][0], swapped[part], momentum, picks, tab, rt, lt4, comp)
        pms.append(pm)
        qs.append(lax.ppermute(q, ("yh", "yl"), NEAR))
    got = lax.all_to_all(comp.reshape(64, 24, 128), REP, 0, 0, tiled=True)
    mine16 = owner(got, irt, ilt)
    every = lax.all_to_all(jnp.broadcast_to(mine16, (64, UROWS, 128)), REP, 0, 0, tiled=True)

    momentum_left = None
    for part in range(PARTS):
        momentum_left = left(part, qs[part], pms[part], picks, rt, lt, irt, ilt, momentum_left)

    other_params = lax.ppermute(params, "c", SWAP)
    other_far = lax.ppermute(far_params, "c", SWAP)
    other_every = lax.ppermute(every, "c", SWAP)
    shape = (2, 16, 2, UROWS, 128)
    update, new = finish(True, me, every.reshape(shape), params, far_params, None)
    (new,) = finish(False, me, other_every.reshape(shape), other_params, other_far, new)
    return momentum_left, update, new.reshape(512, 5120)


def solution(mesh):
    fine = Mesh(mesh.devices.reshape(4, 4, 2, 2, 2), ("x", "z", "yh", "yl", "c"))
    rep, fsdp = ("x", "z", "yh"), ("yl", "c")
    return jax.shard_map(
        body,
        mesh=fine,
        in_specs=(
            P(rep + fsdp, None),
            P(rep + fsdp, None),
            P(rep, fsdp, None),
            P(rep, fsdp, None, None),
            P(fsdp, None),
        ),
        out_specs=(P(rep, fsdp, None), P(fsdp, None), P()),
        check_vma=False,
    )
```

```python
import functools
import math

import jax
import jax.numpy as jnp
import numpy as np
from jax import lax
from jax.experimental import pallas as pl
from jax.experimental.pallas import tpu as pltpu
from jax.sharding import Mesh
from jax.sharding import PartitionSpec as P

KEEP = 16
DECAY = 0.9
STEP = 0.5
PARTS = 2
PAIRS = 8
PER = PAIRS // PARTS
GW = 640
LEFT = 2
QROWS = 656
UROWS = 176
F32 = jnp.float32
BF16 = jnp.bfloat16
I16 = jnp.int16
I32 = jnp.int32
ARB = pltpu.CompilerParams(vmem_limit_bytes=20 * 1024 * 1024)


def cosine():
    k = np.arange(64, dtype=np.float64)[:, None]
    i = np.arange(64, dtype=np.float64)[None, :]
    w = np.where(k == 0, math.sqrt(1.0 / 64), math.sqrt(2.0 / 64))
    return w * np.cos(math.pi * (2.0 * i + 1.0) * k / 128.0)


def halves(m):
    hi = m.astype(np.float32).astype(jnp.bfloat16)
    lo = (m - hi.astype(np.float64)).astype(np.float32).astype(jnp.bfloat16)
    return hi, lo


def diag(m, n):
    return np.kron(np.eye(n), m)


def right_table(m):
    hi, lo = halves(m)
    row = np.concatenate([hi, lo], axis=1)
    return np.concatenate([row, row], axis=0)


def left_table(m):
    return np.concatenate(halves(m), axis=0)


def split(x):
    hi = x.astype(BF16)
    return hi, (x - hi.astype(F32)).astype(BF16)


def mul_right(x, table):
    hi, lo = split(x)
    o = jnp.dot(jnp.concatenate([hi, lo], axis=1), table, preferred_element_type=F32)
    return o[:, :128] + o[:, 128:]


def mul_left(table, x):
    n = table.shape[0] // 2
    hi, lo = split(x)
    o = jnp.dot(table, hi, preferred_element_type=F32)
    return o[:n] + o[n:] + jnp.dot(table[:n], lo, preferred_element_type=F32)


def lanes_of(x, idx):
    return jnp.take_along_axis(x, jnp.broadcast_to(idx, x.shape), axis=1, mode="promise_in_bounds")


def rows_of(x, idx):
    return jnp.take_along_axis(x, idx, axis=0, mode="promise_in_bounds")


def lane(shape):
    return lax.broadcasted_iota(I32, shape, len(shape) - 1)


def sub(shape):
    return lax.broadcasted_iota(I32, shape, 0)


def pow2(e):
    n = e + 100
    r = jnp.full(e.shape, 2.0**-100, F32)
    for bit in range(7):
        r = r * jnp.where((n >> bit) & 1 == 1, 2.0 ** (1 << bit), 1.0)
    r = r * jnp.where((n >> 7) & 1 == 1, 2.0**64, 1.0)
    return r * jnp.where((n >> 7) & 1 == 1, 2.0**64, 1.0)


def exponent(top):
    e = jnp.floor(math.log2(32767.0) - jnp.log(jnp.maximum(top, 1e-35)) * (1 / math.log(2)))
    return jnp.clip(e, -60.0, 99.0).astype(I32)


def coded(x, e):
    v = jnp.floor(x * pow2(e) + 0.5)
    return jnp.clip(v, -32767.0, 32767.0).astype(I32).astype(I16)


def value(q, e):
    return q.astype(I32).astype(F32) * pow2(-e)


def term(hidden, grad, part):
    cols = 5120 // PARTS
    right = lax.slice_in_dim(grad, part * cols, (part + 1) * cols, axis=1)
    return lax.dot_general(hidden, right, (((0,), (0,)), ((), ())), preferred_element_type=F32)


def rows_for(hidden, core):
    yl = lax.axis_index("yl")
    own = lax.dynamic_slice_in_dim(hidden, 128 * (2 * yl + core), 128, axis=1)
    far = lax.dynamic_slice_in_dim(hidden, 128 * (2 * (1 - yl) + core), 128, axis=1)
    return jnp.concatenate([own, far], axis=1)


def place(group, pos):
    return pos if group == 0 else 5 + (pos + 1) % 5


def pick_tables():
    t = np.zeros((2, 8, 128), np.int32)
    for g in range(2):
        for ln in range(128):
            pos = min(ln // 16, 4) if ln < 80 else (ln - 80) % 5
            t[g, 0, ln] = place(g, pos)
            t[g, 1, ln] = 64 * (place(g, pos) % 2) if ln < 80 else 0
    return t


def code_kernel(own, got, q):
    x = (own[...] + got[...]) * (1.0 / 64)
    for p in range(LEFT):
        exps = jnp.zeros((16, 128), I32)
        for t in range(5):
            at = GW * p + 128 * t
            v = x[:, at : at + 128]
            e = exponent(jnp.max(jnp.abs(v), axis=0, keepdims=True))
            q[p, 128 * t : 128 * t + 128, :] = coded(v, e)
            exps = jnp.where(sub((16, 128)) == t, jnp.broadcast_to(e, (16, 128)), exps)
        q[p, 640:656, :] = exps.astype(I16)


def code(own, got):
    spec = pl.BlockSpec((128, LEFT * GW), lambda i: (1, i))
    return pl.pallas_call(
        code_kernel,
        grid=(PER // LEFT,),
        in_specs=[spec, spec],
        out_specs=pl.BlockSpec((LEFT, QROWS, 128), lambda i: (i, 0, 0)),
        out_shape=jax.ShapeDtypeStruct((PER, QROWS, 128), I16),
        compiler_params=ARB,
        cost_estimate=pl.CostEstimate(flops=10**7, bytes_accessed=4 * 2**20, transcendentals=0),
        name="code",
    )(own, got)


def compress_kernel(part, me, own, got, mom, picks, tab, rt, lt, *refs):
    pm, comp = refs[-2:]
    yl = me[0]
    first = 10 * (PER * part + pl.program_id(0))
    ln = lane((1, 128))
    w0 = (own[:128] + got[:128]) * (1.0 / 64) + DECAY * mom[0]
    w1 = (own[128:] + got[128:]) * (1.0 / 64)
    pm[...] = w0
    tiles = []
    for t in range(5):
        tiles += [w0[:, 128 * t : 128 * t + 128], w1[:, 128 * t : 128 * t + 128]]
    o = mul_right(jnp.concatenate(tiles, axis=0), rt[...])
    tiles = [o[256 * t : 256 * t + 256] for t in range(5)]
    u16 = sub((16, 128))
    ln16 = lane((16, 128))
    short = []
    for g in range(2):
        pieces = []
        span = first + tab[g, 0:1, :]
        for rb in range(4):
            qt = picks[rb // 2, rb % 2, 16:32, :]
            chosen = jnp.where(u16 == (ln16 & 15), lanes_of(qt, span), 0)
            idx = jnp.sum(chosen, axis=0, keepdims=True) + tab[g, 1:2, :]
            rows = slice(64 * rb, 64 * rb + 64)
            a = lanes_of(tiles[3 * g][rows], idx)
            b = lanes_of(tiles[3 * g + 1][rows], idx)
            c = lanes_of(tiles[2][rows], idx)
            pieces.append(jnp.where(ln < 32, a, jnp.where(ln < 64, b, c)))
        short.append(jnp.concatenate(pieces, axis=0))
    z = mul_left(lt[...], jnp.concatenate(short, axis=1))
    for g in range(2):
        span = first + tab[g, 0:1, :]
        for rb in range(4):
            rel, a = rb // 2, rb % 2
            to = yl if rel == 0 else 1 - yl
            pt = picks[rel, a, 0:16, :]
            qt = picks[rel, a, 16:32, :]
            pidx, qidx = lanes_of(pt, span), lanes_of(qt, span)
            for h in range(2):
                pi = pidx[8 * h : 8 * h + 8]
                low, high = pi & 7, pi >> 3
                acc = jnp.where(ln < 85, pi, qidx[8 * h : 8 * h + 8]).astype(F32)
                for j in range(8):
                    r = 64 * rb + 8 * j
                    v = rows_of(z[r : r + 8, 128 * g : 128 * g + 128], low)
                    acc = jnp.where((high == j) & (ln < 80), v, acc)
                comp[a, g, to, 8 * h : 8 * h + 8, :] = acc


def compress(part, me, own, got, mom, picks, tab, rt, lt, before):
    n = PER
    full = lambda *s: pl.BlockSpec(s, lambda i, me: (0,) * len(s))
    col = lambda r: pl.BlockSpec((r, GW), lambda i, me: (0, i))
    args = [own, got, mom, picks, tab, rt, lt]
    in_specs = [
        col(256),
        col(256),
        pl.BlockSpec((1, 128, GW), lambda i, me: (0, 0, part * n + i)),
        full(2, 2, 32, 128),
        full(2, 8, 128),
        full(256, 256),
        full(512, 256),
    ]
    alias = {}
    if before is not None:
        args.append(before)
        in_specs.append(pl.BlockSpec(memory_space=pl.ANY))
        alias = {8: 1}
    return pl.pallas_call(
        functools.partial(compress_kernel, part),
        grid_spec=pltpu.PrefetchScalarGridSpec(
            num_scalar_prefetch=1,
            grid=(n,),
            in_specs=in_specs,
            out_specs=[
                col(128),
                pl.BlockSpec((2, 2, 2, 16, 128), lambda i, me: (0, part * n + i, 0, 0, 0)),
            ],
        ),
        out_shape=[
            jax.ShapeDtypeStruct((128, 5120 // PARTS), F32),
            jax.ShapeDtypeStruct((2, 16, 2, 16, 128), F32),
        ],
        input_output_aliases=alias,
        compiler_params=ARB,
        cost_estimate=pl.CostEstimate(flops=2 * 10**9, bytes_accessed=9 * 2**20, transcendentals=0),
        name="compress",
    )(me, *args)


def owner_kernel(got, rt, lt, out, xh, xl, hot):
    ln16 = lane((16, 128))

    here = (ln16 & 63).astype(F32)
    u16 = sub((16, 128))

    def one(n, _):
        at = pl.multiple_of(16 * n, 16)
        x = got[n]
        for t in range(3):
            half = 2 * t + (ln16 >> 6)
            hit = jnp.where(lanes_of(x, 85 + half) == here, 16 * half + u16 + 1, 0)
            if t == 2:
                hit = jnp.where(ln16 < 64, hit, 0)
            idx = jnp.broadcast_to(jnp.sum(hit, axis=0, keepdims=True), (16, 128)) - 1
            v = jnp.where(idx >= 0, lanes_of(x, jnp.maximum(idx, 0)), 0.0)
            hi, lo = split(v)
            xh[t, pl.ds(at, 16), :] = hi
            xl[t, pl.ds(at, 16), :] = lo
            hot[t, pl.ds(at, 16), :] = jnp.where(lanes_of(x, 80 + half) == here, 1.0, 0.0).astype(BF16)
        return 0

    lax.fori_loop(0, got.shape[0], one, 0, unroll=4)
    same = (sub((128, 128)) >> 6) == (lane((128, 128)) >> 6)
    tiles = []
    for t in range(3):
        dims = (((0,), (0,)), ((), ()))
        d = lax.dot_general(hot[t], xh[t], dims, preferred_element_type=F32)
        d = d + lax.dot_general(hot[t], xl[t], dims, preferred_element_type=F32)
        d = jnp.where(same, d, 0.0)
        u = mul_left(lt[...], mul_right(d, rt[...]))
        tiles.append(u[:64] + u[64:])
    last = tiles[2]
    ln = lane((32, 128))
    tiles[2] = jnp.where(ln < 64, last[:32], jnp.roll(last[32:], 64, axis=1))
    x = jnp.concatenate(tiles, axis=0)
    e = exponent(jnp.max(jnp.abs(x), axis=0, keepdims=True))
    out[0:160, :] = coded(x, e)
    out[160:176, :] = jnp.broadcast_to(e, (16, 128)).astype(I16)


def owner(got, rt, lt):
    return pl.pallas_call(
        owner_kernel,
        out_shape=jax.ShapeDtypeStruct((UROWS, 128), I16),
        scratch_shapes=[pltpu.VMEM((3, 1024, 128), BF16)] * 3,
        compiler_params=ARB,
        name="owner",
    )(got, rt, lt)


def decode(ref, pair):
    group = []
    for g in (2 * pair, 2 * pair + 1):
        e = ref[g, 160:176, :].astype(I32)[:1]
        group.append(value(ref[g, 0:160, :], e))
    even, odd = group
    lo = lane((32, 128)) < 64
    e2, o2 = even[128:160], odd[128:160]
    top = jnp.where(lo, e2, jnp.roll(o2, 64, axis=1))
    bottom = jnp.where(lo, jnp.roll(e2, 64, axis=1), o2)
    return [even[:64], even[64:128], jnp.concatenate([top, bottom], axis=0), odd[:64], odd[64:128]]


def finish_kernel(with_update, _, got0, got1, par, *refs):
    for a, got in enumerate((got0, got1)):
        rows = slice(64 * a, 64 * a + 64)
        for pair in range(LEFT):
            for t, u in enumerate(decode(got, pair)):
                cols = slice(GW * pair + 128 * t, GW * pair + 128 * t + 128)
                if with_update:
                    refs[-2][rows, cols] = u
                refs[-1][rows, cols] = (par[rows, cols].astype(F32) - STEP * u).astype(BF16)


def finish(row, got0, got1, par, before):
    with_update = before is None
    col = pl.BlockSpec((128, LEFT * GW), lambda i, row: (0, i))
    blocks = pl.BlockSpec((2 * LEFT, UROWS, 128), lambda i, row: (i, 0, 0))
    args = [got0, got1, par]
    in_specs = [blocks, blocks, col]
    out_specs = [pl.BlockSpec((128, LEFT * GW), lambda i, row: (row[0], i))]
    out_shape = [jax.ShapeDtypeStruct((512, 5120), BF16)]
    alias = {}
    if with_update:
        out_specs.insert(0, col)
        out_shape.insert(0, jax.ShapeDtypeStruct((128, 5120), F32))
    else:
        args.append(before)
        in_specs.append(pl.BlockSpec(memory_space=pl.ANY))
        alias = {4: 0}
    return pl.pallas_call(
        functools.partial(finish_kernel, with_update),
        grid_spec=pltpu.PrefetchScalarGridSpec(
            num_scalar_prefetch=1, grid=(PAIRS // LEFT,), in_specs=in_specs, out_specs=out_specs
        ),
        out_shape=out_shape,
        input_output_aliases=alias,
        compiler_params=ARB,
        cost_estimate=pl.CostEstimate(flops=10**7, bytes_accessed=4 * 2**20, transcendentals=0),
        name="finish",
    )(row, *args)


def left_kernel(part, q, pm, picks, rt, lt, irt, ilt, *refs):
    out, mask = refs[-2:]
    first = 10 * (PER * part + LEFT * pl.program_id(0))

    @pl.when(pl.program_id(0) == 0)
    def _():
        for a in range(2):
            k = sub((64, 128))
            hit = jnp.zeros((64, 128), F32)
            for u in range(16):
                hit = jnp.where(picks[0, a, u : u + 1, :] == k, 1.0, hit)
            mask[64 * a : 64 * a + 64, :] = hit

    ln16 = lane((16, 128))
    rows = sub((128, 128)) < 64
    moment, keep = [], []
    for t in range(5 * LEFT):
        e = q[t // 5, 640:656, :].astype(I32)[t % 5 : t % 5 + 1]
        at = 128 * (t % 5)
        moment.append(pm[:, 128 * t : 128 * t + 128] + value(q[t // 5, at : at + 128, :], e))
        span = first + 2 * t + (lane((1, 128)) >> 6)
        both = []
        for a in range(2):
            hit = lanes_of(picks[0, a, 16:32, :], span) == (ln16 & 63)
            both.append(jnp.max(jnp.where(hit, 1.0, 0.0), axis=0, keepdims=True))
        keep.append(lanes_of(mask[...], span) * jnp.where(rows, both[0], both[1]))
    n = len(moment)
    c = mul_right(jnp.concatenate(moment, axis=0), rt[...])
    c = mul_left(lt[...], jnp.concatenate([c[128 * t : 128 * t + 128] for t in range(n)], axis=1))
    c = mul_left(ilt[...], c * jnp.concatenate(keep, axis=1))
    r = mul_right(jnp.concatenate([c[:, 128 * t : 128 * t + 128] for t in range(n)], axis=0), irt[...])
    for t in range(n):
        out[0, :, 128 * t : 128 * t + 128] = moment[t] - r[128 * t : 128 * t + 128]


def left(part, q, pm, picks, rt, lt, irt, ilt, before):
    n = PER // LEFT
    full = lambda *s: pl.BlockSpec(s, lambda i: (0,) * len(s))
    args = [q, pm, picks, rt, lt, irt, ilt]
    in_specs = [
        pl.BlockSpec((LEFT, QROWS, 128), lambda i: (i, 0, 0)),
        pl.BlockSpec((128, LEFT * GW), lambda i: (0, i)),
        full(2, 2, 32, 128),
        full(256, 256),
        full(256, 128),
        full(256, 256),
        full(256, 128),
    ]
    alias = {}
    if before is not None:
        args.append(before)
        in_specs.append(pl.BlockSpec(memory_space=pl.ANY))
        alias = {7: 0}
    return pl.pallas_call(
        functools.partial(left_kernel, part),
        grid=(n,),
        in_specs=in_specs,
        out_specs=pl.BlockSpec((1, 128, LEFT * GW), lambda i: (0, 0, part * n + i)),
        out_shape=jax.ShapeDtypeStruct((1, 128, 5120), F32),
        scratch_shapes=[pltpu.VMEM((128, 128), F32)],
        input_output_aliases=alias,
        compiler_params=ARB,
        cost_estimate=pl.CostEstimate(flops=2 * 10**9, bytes_accessed=4 * 2**20, transcendentals=0),
        name="left",
    )(*args)


REP = ("x", "z", "yh")
NEAR = [(2 * h + k, 2 * h + 1 - k) for h in range(2) for k in range(2)]
FAR = [(y, 3 - y) for y in range(4)]
SWAP = [(0, 1), (1, 0)]


def body(hidden, grad, momentum, coef_picks, params):
    c = cosine()
    rt = jnp.asarray(right_table(diag(c.T, 2)))
    irt = jnp.asarray(right_table(diag(c, 2)))
    lt4 = jnp.asarray(left_table(diag(c, 4)))
    lt = jnp.asarray(left_table(diag(c, 2)))
    ilt = jnp.asarray(left_table(diag(c.T, 2)))
    tab = jnp.asarray(pick_tables())
    me = jnp.stack([lax.axis_index("yl"), lax.axis_index("c")]).astype(I32)

    mine = jnp.pad(coef_picks[0].swapaxes(1, 2), ((0, 0), (0, 0), (0, 48)))
    theirs = lax.ppermute(mine, ("yh", "yl"), NEAR)
    picks = jnp.stack([mine, theirs])
    far_params = lax.ppermute(params, ("yh", "yl"), FAR)

    core = lax.axis_index("c")
    sent = rows_for(hidden, 1 - core)
    kept = rows_for(hidden, core)
    swapped = [lax.ppermute(term(sent, grad, part), "c", SWAP) for part in range(PARTS)]
    own = [term(kept, grad, part) for part in range(PARTS)]
    qs = [lax.ppermute(code(own[p], swapped[p]), ("yh", "yl"), NEAR) for p in range(PARTS)]
    pms, comp = [], None
    for part in range(PARTS):
        pm, comp = compress(part, me, own[part], swapped[part], momentum, picks, tab, rt, lt4, comp)
        pms.append(pm)
    comp, qs[0] = lax.optimization_barrier((comp, qs[0]))
    got = lax.all_to_all(comp.reshape(64, 16, 128), REP + ("yl",), 0, 0, tiled=True)
    first_left = left(0, qs[0], pms[0], picks, rt, lt, irt, ilt, None)
    got, first_left = lax.optimization_barrier((got, first_left))
    mine16 = owner(got, irt, ilt)
    other_params = lax.ppermute(params, "c", SWAP)
    mine16, qs[1], far_params, other_params = lax.optimization_barrier((mine16, qs[1], far_params, other_params))
    other_far = lax.ppermute(far_params, "c", SWAP)
    every = lax.all_to_all(jnp.broadcast_to(mine16, (32, UROWS, 128)), REP, 0, 0, tiled=True)

    block = [every[:16], every[16:]]
    far = [lax.ppermute(v, ("yh", "yl"), way) for v, way in zip(block, (NEAR, FAR))]
    other = [lax.ppermute(v, "c", SWAP) for v in block]
    momentum_left = left(1, qs[1], pms[1], picks, rt, lt, irt, ilt, first_left)
    row = lambda y, c: (2 * y + c).astype(I32).reshape(1)
    yl = lax.axis_index("yl")
    update, new = finish(row(yl, core), *block, params, None)
    (new,) = finish(row(yl, 1 - core), *other, other_params, new)
    far, new, momentum_left = lax.optimization_barrier((far, new, momentum_left))
    other_distant = [lax.ppermute(v, "c", SWAP) for v in far]
    (new,) = finish(row(1 - yl, core), *far, far_params, new)
    (new,) = finish(row(1 - yl, 1 - core), *other_distant, other_far, new)
    return momentum_left, update, new


def solution(mesh):
    fine = Mesh(mesh.devices.reshape(4, 4, 2, 2, 2), ("x", "z", "yh", "yl", "c"))
    rep, fsdp = ("x", "z", "yh"), ("yl", "c")
    return jax.shard_map(
        body,
        mesh=fine,
        in_specs=(
            P(rep + fsdp, None),
            P(rep + fsdp, None),
            P(rep, fsdp, None),
            P(rep, fsdp, None, None),
            P(fsdp, None),
        ),
        out_specs=(P(rep, fsdp, None), P(fsdp, None), P()),
        check_vma=False,
    )
```

```python
import functools
import math

import jax
import jax.numpy as jnp
import numpy as np
from jax import lax
from jax.experimental import pallas as pl
from jax.experimental.pallas import tpu as pltpu
from jax.sharding import Mesh
from jax.sharding import PartitionSpec as P

KEEP = 16
DECAY = 0.9
STEP = 0.5
PARTS = 2
PAIRS = 8
PER = PAIRS // PARTS
GW = 640
LEFT = 2
QROWS = 656
UROWS = 176
F32 = jnp.float32
BF16 = jnp.bfloat16
I16 = jnp.int16
I32 = jnp.int32
ARB = pltpu.CompilerParams(vmem_limit_bytes=20 * 1024 * 1024)


SHORT = pl.CostEstimate(flops=1000, bytes_accessed=1000, transcendentals=0)


def cosine():
    k = np.arange(64, dtype=np.float64)[:, None]
    i = np.arange(64, dtype=np.float64)[None, :]
    w = np.where(k == 0, math.sqrt(1.0 / 64), math.sqrt(2.0 / 64))
    return w * np.cos(math.pi * (2.0 * i + 1.0) * k / 128.0)


def halves(m):
    hi = m.astype(np.float32).astype(jnp.bfloat16)
    lo = (m - hi.astype(np.float64)).astype(np.float32).astype(jnp.bfloat16)
    return hi, lo


def diag(m, n):
    return np.kron(np.eye(n), m)


def right_table(m):
    hi, lo = halves(m)
    row = np.concatenate([hi, lo], axis=1)
    return np.concatenate([row, row], axis=0)


def left_table(m):
    return np.concatenate(halves(m), axis=0)


def split(x):
    hi = x.astype(BF16)
    return hi, (x - hi.astype(F32)).astype(BF16)


def mul_right(x, table):
    hi, lo = split(x)
    o = jnp.dot(jnp.concatenate([hi, lo], axis=1), table, preferred_element_type=F32)
    return o[:, :128] + o[:, 128:]


def mul_left(table, x):
    n = table.shape[0] // 2
    hi, lo = split(x)
    o = jnp.dot(table, hi, preferred_element_type=F32)
    return o[:n] + o[n:] + jnp.dot(table[:n], lo, preferred_element_type=F32)


def lanes_of(x, idx):
    return jnp.take_along_axis(x, jnp.broadcast_to(idx, x.shape), axis=1, mode="promise_in_bounds")


def rows_of(x, idx):
    return jnp.take_along_axis(x, idx, axis=0, mode="promise_in_bounds")


def lane(shape):
    return lax.broadcasted_iota(I32, shape, len(shape) - 1)


def sub(shape):
    return lax.broadcasted_iota(I32, shape, 0)


def pow2(e):
    n = e + 100
    r = jnp.full(e.shape, 2.0**-100, F32)
    for bit in range(7):
        r = r * jnp.where((n >> bit) & 1 == 1, 2.0 ** (1 << bit), 1.0)
    r = r * jnp.where((n >> 7) & 1 == 1, 2.0**64, 1.0)
    return r * jnp.where((n >> 7) & 1 == 1, 2.0**64, 1.0)


def exponent(top):
    e = jnp.floor(math.log2(32767.0) - jnp.log(jnp.maximum(top, 1e-35)) * (1 / math.log(2)))
    return jnp.clip(e, -60.0, 99.0).astype(I32)


def coded(x, e):
    v = jnp.floor(x * pow2(e) + 0.5)
    return jnp.clip(v, -32767.0, 32767.0).astype(I32).astype(I16)


def value(q, e):
    return q.astype(I32).astype(F32) * pow2(-e)


def term(hidden, grad, part):
    cols = 5120 // PARTS
    right = lax.slice_in_dim(grad, part * cols, (part + 1) * cols, axis=1)
    return lax.dot_general(hidden, right, (((0,), (0,)), ((), ())), preferred_element_type=F32)


def rows_for(hidden, core):
    yl = lax.axis_index("yl")
    own = lax.dynamic_slice_in_dim(hidden, 128 * (2 * yl + core), 128, axis=1)
    far = lax.dynamic_slice_in_dim(hidden, 128 * (2 * (1 - yl) + core), 128, axis=1)
    return jnp.concatenate([own, far], axis=1)


def place(group, pos):
    return pos if group == 0 else 5 + (pos + 1) % 5


def pick_tables():
    t = np.zeros((2, 8, 128), np.int32)
    for g in range(2):
        for ln in range(128):
            pos = min(ln // 16, 4) if ln < 80 else (ln - 80) % 5
            t[g, 0, ln] = place(g, pos)
            t[g, 1, ln] = 64 * (place(g, pos) % 2) if ln < 80 else 0
    return t


def code(x, q):
    for p in range(LEFT):
        exps = jnp.zeros((16, 128), I32)
        for t in range(5):
            at = GW * p + 128 * t
            v = x[:, at : at + 128]
            e = exponent(jnp.max(jnp.abs(v), axis=0, keepdims=True))
            q[p, 128 * t : 128 * t + 128, :] = coded(v, e)
            exps = jnp.where(sub((16, 128)) == t, jnp.broadcast_to(e, (16, 128)), exps)
        q[p, 640:656, :] = exps.astype(I16)


def code_kernel(own, got, q):
    code((own[...] + got[...]) * (1.0 / 64), q)


def code_alone(own, got):
    spec = pl.BlockSpec((128, LEFT * GW), lambda i: (1, i))
    return pl.pallas_call(
        code_kernel,
        grid=(PER // LEFT,),
        in_specs=[spec, spec],
        out_specs=pl.BlockSpec((LEFT, QROWS, 128), lambda i: (i, 0, 0)),
        out_shape=jax.ShapeDtypeStruct((PER, QROWS, 128), I16),
        compiler_params=ARB,
        cost_estimate=SHORT,
        name="code",
    )(own, got)


def compress_kernel(part, with_code, me, own, got, mom, picks, tab, rt, lt, *refs):
    pm, comp = refs[-2:]
    yl = me[0]
    first = 10 * (PER * part + LEFT * pl.program_id(0))
    ln = lane((1, 128))
    w0 = (own[:128] + got[:128]) * (1.0 / 64) + DECAY * mom[0]
    w1 = (own[128:] + got[128:]) * (1.0 / 64)
    pm[...] = w0
    if with_code:
        code(w1, refs[-3])
    tiles = []
    for t in range(5 * LEFT):
        tiles += [w0[:, 128 * t : 128 * t + 128], w1[:, 128 * t : 128 * t + 128]]
    o = mul_right(jnp.concatenate(tiles, axis=0), rt[...])
    tiles = [o[256 * t : 256 * t + 256] for t in range(5 * LEFT)]
    u16 = sub((16, 128))
    ln16 = lane((16, 128))
    short = []
    for k in range(2 * LEFT):
        g, at = k % 2, 5 * (k // 2)
        pieces = []
        span = first + 2 * at + tab[g, 0:1, :]
        for rb in range(4):
            qt = picks[rb // 2, rb % 2, 16:32, :]
            chosen = jnp.where(u16 == (ln16 & 15), lanes_of(qt, span), 0)
            idx = jnp.sum(chosen, axis=0, keepdims=True) + tab[g, 1:2, :]
            rows = slice(64 * rb, 64 * rb + 64)
            a = lanes_of(tiles[at + 3 * g][rows], idx)
            b = lanes_of(tiles[at + 3 * g + 1][rows], idx)
            c = lanes_of(tiles[at + 2][rows], idx)
            pieces.append(jnp.where(ln < 32, a, jnp.where(ln < 64, b, c)))
        short.append(jnp.concatenate(pieces, axis=0))
    z = mul_left(lt[...], jnp.concatenate(short, axis=1))
    for k in range(2 * LEFT):
        span = first + 10 * (k // 2) + tab[k % 2, 0:1, :]
        for rb in range(4):
            rel, a = rb // 2, rb % 2
            to = yl if rel == 0 else 1 - yl
            pt = picks[rel, a, 0:16, :]
            qt = picks[rel, a, 16:32, :]
            pidx, qidx = lanes_of(pt, span), lanes_of(qt, span)
            for h in range(2):
                pi = pidx[8 * h : 8 * h + 8]
                low, high = pi & 7, pi >> 3
                acc = jnp.where(ln < 85, pi, qidx[8 * h : 8 * h + 8]).astype(F32)
                for j in range(8):
                    r = 64 * rb + 8 * j
                    v = rows_of(z[r : r + 8, 128 * k : 128 * k + 128], low)
                    acc = jnp.where((high == j) & (ln < 80), v, acc)
                comp[a, k, to, 8 * h : 8 * h + 8, :] = acc


def compress(part, with_code, me, own, got, mom, picks, tab, rt, lt, before):
    n = PER // LEFT
    full = lambda *s: pl.BlockSpec(s, lambda i, me: (0,) * len(s))
    col = lambda r: pl.BlockSpec((r, LEFT * GW), lambda i, me: (0, i))
    args = [own, got, mom, picks, tab, rt, lt]
    in_specs = [
        col(256),
        col(256),
        pl.BlockSpec((1, 128, LEFT * GW), lambda i, me: (0, 0, part * n + i)),
        full(2, 2, 32, 128),
        full(2, 8, 128),
        full(256, 256),
        full(512, 256),
    ]
    alias = {}
    if before is not None:
        args.append(before)
        in_specs.append(pl.BlockSpec(memory_space=pl.ANY))
        alias = {8: 1 + with_code}
    return pl.pallas_call(
        functools.partial(compress_kernel, part, with_code),
        grid_spec=pltpu.PrefetchScalarGridSpec(
            num_scalar_prefetch=1,
            grid=(n,),
            in_specs=in_specs,
            out_specs=([pl.BlockSpec((LEFT, QROWS, 128), lambda i, me: (i, 0, 0))] if with_code else [])
            + [col(128), pl.BlockSpec((2, 2 * LEFT, 2, 16, 128), lambda i, me: (0, part * n + i, 0, 0, 0))],
        ),
        out_shape=([jax.ShapeDtypeStruct((PER, QROWS, 128), I16)] if with_code else [])
        + [
            jax.ShapeDtypeStruct((128, 5120 // PARTS), F32),
            jax.ShapeDtypeStruct((2, 16, 2, 16, 128), F32),
        ],
        input_output_aliases=alias,
        compiler_params=ARB,
        cost_estimate=SHORT,
        name="compress",
    )(me, *args)


def owner_kernel(got, rt, lt, out, xs, hot):
    ln16 = lane((16, 128))

    here = (ln16 & 63).astype(F32)
    u16 = sub((16, 128))

    def one(n, _):
        at = pl.multiple_of(16 * n, 16)
        x = got[2 * n]
        x = jnp.where(ln16 < 80, x + got[2 * n + 1], x)
        for t in range(3):
            half = 2 * t + (ln16 >> 6)
            hit = jnp.where(lanes_of(x, 85 + half) == here, 16 * half + u16 + 1, 0)
            if t == 2:
                hit = jnp.where(ln16 < 64, hit, 0)
            idx = jnp.broadcast_to(jnp.sum(hit, axis=0, keepdims=True), (16, 128)) - 1
            v = jnp.where(idx >= 0, lanes_of(x, jnp.maximum(idx, 0)), 0.0)
            hi, lo = split(v)
            xs[t, pl.ds(at, 16), :] = jnp.concatenate([hi, lo], axis=1)
            hot[t, pl.ds(at, 16), :] = jnp.where(lanes_of(x, 80 + half) == here, 1.0, 0.0).astype(BF16)
        return 0

    lax.fori_loop(0, got.shape[0] // 2, one, 0, unroll=8)
    same = (sub((128, 128)) >> 6) == (lane((128, 128)) >> 6)
    grids = []
    for t in range(3):
        d = lax.dot_general(hot[t], xs[t], (((0,), (0,)), ((), ())), preferred_element_type=F32)
        grids.append(jnp.where(same, d[:, :128] + d[:, 128:], 0.0))
    d = mul_right(jnp.concatenate(grids, axis=0), rt[...])
    u = mul_left(lt[...], jnp.concatenate([d[128 * t : 128 * t + 128] for t in range(3)], axis=1))
    u = u[:64] + u[64:]
    tiles = [u[:, 128 * t : 128 * t + 128] for t in range(3)]
    last = tiles[2]
    ln = lane((32, 128))
    tiles[2] = jnp.where(ln < 64, last[:32], jnp.roll(last[32:], 64, axis=1))
    x = jnp.concatenate(tiles, axis=0)
    e = exponent(jnp.max(jnp.abs(x), axis=0, keepdims=True))
    out[0:160, :] = coded(x, e)
    out[160:176, :] = jnp.broadcast_to(e, (16, 128)).astype(I16)


def owner(got, rt, lt):
    return pl.pallas_call(
        owner_kernel,
        out_shape=jax.ShapeDtypeStruct((UROWS, 128), I16),
        scratch_shapes=[pltpu.VMEM((3, 512, 256), BF16), pltpu.VMEM((3, 512, 128), BF16)],
        compiler_params=ARB,
        name="owner",
    )(got, rt, lt)


def decode(ref, pair):
    group = []
    for g in (2 * pair, 2 * pair + 1):
        e = ref[g, 160:176, :].astype(I32)[:1]
        group.append(value(ref[g, 0:160, :], e))
    even, odd = group
    lo = lane((32, 128)) < 64
    e2, o2 = even[128:160], odd[128:160]
    top = jnp.where(lo, e2, jnp.roll(o2, 64, axis=1))
    bottom = jnp.where(lo, jnp.roll(e2, 64, axis=1), o2)
    return [even[:64], even[64:128], jnp.concatenate([top, bottom], axis=0), odd[:64], odd[64:128]]


def finish_kernel(got, par, *refs):
    update, new = refs[-2:]
    for pair in range(LEFT):
        for t, u in enumerate(decode(got, pair)):
            cols = slice(GW * pair + 128 * t, GW * pair + 128 * t + 128)
            update[:, cols] = u
            new[:, cols] = (par[:, cols].astype(F32) - STEP * u).astype(BF16)


def finish(a, got, par, before):
    n = PAIRS // LEFT
    half = pl.BlockSpec((64, LEFT * GW), lambda i: (a, i))
    args = [got, par]
    in_specs = [pl.BlockSpec((2 * LEFT, UROWS, 128), lambda i: (n * a + i, 0, 0)), half]
    alias = {}
    if before is not None:
        args.append(before)
        in_specs.append(pl.BlockSpec(memory_space=pl.ANY))
        alias = {2: 0}
    return pl.pallas_call(
        finish_kernel,
        grid=(n,),
        in_specs=in_specs,
        out_specs=[half, pl.BlockSpec((64, LEFT * GW), lambda i: (0, i))],
        out_shape=[jax.ShapeDtypeStruct((128, 5120), F32), jax.ShapeDtypeStruct((64, 5120), BF16)],
        input_output_aliases=alias,
        compiler_params=ARB,
        cost_estimate=SHORT,
        name="finish",
    )(*args)


def gather_kernel(n, rows, *refs):
    sem = refs[-1]
    out = refs[-2]
    copies = []
    for i in range(n):
        for k in range(4):
            at = pl.multiple_of(rows[i] + 16 * k, 16)
            copies.append(
                pltpu.make_async_copy(refs[i].at[16 * k : 16 * k + 16, :], out.at[pl.ds(at, 16), :], sem.at[4 * i + k])
            )
            copies[-1].start()
    for copy in copies:
        copy.wait()


def gather(rows, parts, before):
    n = len(parts)
    anywhere = pl.BlockSpec(memory_space=pl.ANY)
    args = list(parts) + ([] if before is None else [before])
    return pl.pallas_call(
        functools.partial(gather_kernel, n),
        grid_spec=pltpu.PrefetchScalarGridSpec(
            num_scalar_prefetch=1,
            grid=(1,),
            in_specs=[anywhere] * len(args),
            out_specs=anywhere,
            scratch_shapes=[pltpu.SemaphoreType.DMA((4 * n,))],
        ),
        out_shape=jax.ShapeDtypeStruct((512, 5120), BF16),
        input_output_aliases={} if before is None else {n + 1: 0},
        compiler_params=ARB,
        cost_estimate=pl.CostEstimate(flops=0, bytes_accessed=4 * 2**20, transcendentals=0),
        name="gather",
    )(rows, *args)


def left_kernel(part, q, pm, picks, rt, lt, irt, ilt, *refs):
    out, mask = refs[-2:]
    first = 10 * (PER * part + LEFT * pl.program_id(0))

    @pl.when(pl.program_id(0) == 0)
    def _():
        for a in range(2):
            k = sub((64, 128))
            hit = jnp.zeros((64, 128), F32)
            for u in range(16):
                hit = jnp.where(picks[0, a, u : u + 1, :] == k, 1.0, hit)
            mask[64 * a : 64 * a + 64, :] = hit

    ln16 = lane((16, 128))
    rows = sub((128, 128)) < 64
    moment, keep = [], []
    for t in range(5 * LEFT):
        e = q[t // 5, 640:656, :].astype(I32)[t % 5 : t % 5 + 1]
        at = 128 * (t % 5)
        moment.append(pm[:, 128 * t : 128 * t + 128] + value(q[t // 5, at : at + 128, :], e))
        span = first + 2 * t + (lane((1, 128)) >> 6)
        both = []
        for a in range(2):
            hit = lanes_of(picks[0, a, 16:32, :], span) == (ln16 & 63)
            both.append(jnp.max(jnp.where(hit, 1.0, 0.0), axis=0, keepdims=True))
        keep.append(lanes_of(mask[...], span) * jnp.where(rows, both[0], both[1]))
    n = len(moment)
    c = mul_right(jnp.concatenate(moment, axis=0), rt[...])
    c = mul_left(lt[...], jnp.concatenate([c[128 * t : 128 * t + 128] for t in range(n)], axis=1))
    c = mul_left(ilt[...], c * jnp.concatenate(keep, axis=1))
    r = mul_right(jnp.concatenate([c[:, 128 * t : 128 * t + 128] for t in range(n)], axis=0), irt[...])
    for t in range(n):
        out[0, :, 128 * t : 128 * t + 128] = moment[t] - r[128 * t : 128 * t + 128]


def left(part, q, pm, picks, rt, lt, irt, ilt, before):
    n = PER // LEFT
    full = lambda *s: pl.BlockSpec(s, lambda i: (0,) * len(s))
    args = [q, pm, picks, rt, lt, irt, ilt]
    in_specs = [
        pl.BlockSpec((LEFT, QROWS, 128), lambda i: (i, 0, 0)),
        pl.BlockSpec((128, LEFT * GW), lambda i: (0, i)),
        full(2, 2, 32, 128),
        full(256, 256),
        full(256, 128),
        full(256, 256),
        full(256, 128),
    ]
    alias = {}
    if before is not None:
        args.append(before)
        in_specs.append(pl.BlockSpec(memory_space=pl.ANY))
        alias = {7: 0}
    return pl.pallas_call(
        functools.partial(left_kernel, part),
        grid=(n,),
        in_specs=in_specs,
        out_specs=pl.BlockSpec((1, 128, LEFT * GW), lambda i: (0, 0, part * n + i)),
        out_shape=jax.ShapeDtypeStruct((1, 128, 5120), F32),
        scratch_shapes=[pltpu.VMEM((128, 128), F32)],
        input_output_aliases=alias,
        compiler_params=ARB,
        cost_estimate=SHORT,
        name="left",
    )(*args)


REP = ("x", "z", "yh")
NEAR = [(2 * h + k, 2 * h + 1 - k) for h in range(2) for k in range(2)]
FAR = [(y, 3 - y) for y in range(4)]
SWAP = [(0, 1), (1, 0)]


def body(hidden, grad, momentum, coef_picks, params):
    c = cosine()
    rt = jnp.asarray(right_table(diag(c.T, 2)))
    irt = jnp.asarray(right_table(diag(c, 2)))
    lt4 = jnp.asarray(left_table(diag(c, 4)))
    lt = jnp.asarray(left_table(diag(c, 2)))
    ilt = jnp.asarray(left_table(diag(c.T, 2)))
    tab = jnp.asarray(pick_tables())
    me = jnp.stack([lax.axis_index("yl"), lax.axis_index("c")]).astype(I32)

    mine = jnp.pad(coef_picks[0].swapaxes(1, 2), ((0, 0), (0, 0), (0, 48)))
    theirs = lax.ppermute(mine, ("yh", "yl"), NEAR)
    picks = jnp.stack([mine, theirs])

    core = lax.axis_index("c")
    sent = rows_for(hidden, 1 - core)
    kept = rows_for(hidden, core)
    swapped = [lax.ppermute(term(sent, grad, part), "c", SWAP) for part in range(PARTS)]
    own = [term(kept, grad, part) for part in range(PARTS)]
    tables = (momentum, picks, tab, rt, lt4)
    q0 = lax.ppermute(code_alone(own[0], swapped[0]), ("yh", "yl"), NEAR)
    pm0, comp = compress(0, False, me, own[0], swapped[0], *tables, None)
    q1, pm1, comp = compress(1, True, me, own[1], swapped[1], *tables, comp)
    q1 = lax.ppermute(q1, ("yh", "yl"), NEAR)
    comp, q0 = lax.optimization_barrier((comp, q0))
    got = lax.all_to_all(comp.reshape(64, 16, 128), REP + ("yl",), 0, 0, tiled=True)
    momentum_left = left(0, q0, pm0, picks, rt, lt, irt, ilt, None)
    got, momentum_left = lax.optimization_barrier((got, momentum_left))
    mine16 = owner(got, irt, ilt)
    mine16, q1 = lax.optimization_barrier((mine16, q1))
    every = lax.all_to_all(jnp.broadcast_to(mine16, (32, UROWS, 128)), REP, 0, 0, tiled=True)
    every, pm1 = lax.optimization_barrier((every, pm1))

    yl = lax.axis_index("yl")
    rows = lambda y, c: (128 * (2 * y + c) + 64 * jnp.arange(2)).astype(I32)
    update, low = finish(0, every, params, None)
    far_low = lax.ppermute(low, ("yh", "yl"), NEAR)
    update, high = finish(1, every, params, update)
    far_high = lax.ppermute(high, ("yh", "yl"), FAR)
    momentum_left = left(1, q1, pm1, picks, rt, lt, irt, ilt, momentum_left)
    other = [lax.ppermute(v, "c", SWAP) for v in (low, high)]
    where = jnp.concatenate([rows(yl, core), rows(yl, 1 - core)])
    new = gather(where, [low, high, *other], None)
    far_low, far_high, new, momentum_left = lax.optimization_barrier((far_low, far_high, new, momentum_left))
    distant = [lax.ppermute(v, "c", SWAP) for v in (far_low, far_high)]
    new = gather(rows(1 - yl, core), [far_low, far_high], new)
    distant, new = lax.optimization_barrier((distant, new))
    new = gather(rows(1 - yl, 1 - core), distant, new)
    return momentum_left, update, new


def solution(mesh):
    fine = Mesh(mesh.devices.reshape(4, 4, 2, 2, 2), ("x", "z", "yh", "yl", "c"))
    rep, fsdp = ("x", "z", "yh"), ("yl", "c")
    return jax.shard_map(
        body,
        mesh=fine,
        in_specs=(
            P(rep + fsdp, None),
            P(rep + fsdp, None),
            P(rep, fsdp, None),
            P(rep, fsdp, None, None),
            P(fsdp, None),
        ),
        out_specs=(P(rep, fsdp, None), P(fsdp, None), P()),
        check_vma=False,
    )
```

```python
import functools
import math

import jax
import jax.numpy as jnp
import numpy as np
from jax import lax
from jax.experimental import pallas as pl
from jax.experimental.pallas import tpu as pltpu
from jax.sharding import Mesh
from jax.sharding import PartitionSpec as P

KEEP = 16
DECAY = 0.9
STEP = 0.5
PARTS = 2
PAIRS = 8
PER = PAIRS // PARTS
GW = 640
LEFT = 2
QROWS = 656
UROWS = 176
F32 = jnp.float32
BF16 = jnp.bfloat16
I16 = jnp.int16
I32 = jnp.int32
ARB = pltpu.CompilerParams(vmem_limit_bytes=20 * 1024 * 1024)


SHORT = pl.CostEstimate(flops=1000, bytes_accessed=1000, transcendentals=0)


def cosine():
    k = np.arange(64, dtype=np.float64)[:, None]
    i = np.arange(64, dtype=np.float64)[None, :]
    w = np.where(k == 0, math.sqrt(1.0 / 64), math.sqrt(2.0 / 64))
    return w * np.cos(math.pi * (2.0 * i + 1.0) * k / 128.0)


def halves(m):
    hi = m.astype(np.float32).astype(jnp.bfloat16)
    lo = (m - hi.astype(np.float64)).astype(np.float32).astype(jnp.bfloat16)
    return hi, lo


def diag(m, n):
    return np.kron(np.eye(n), m)


def right_table(m):
    hi, lo = halves(m)
    row = np.concatenate([hi, lo], axis=1)
    return np.concatenate([row, row], axis=0)


def left_table(m):
    return np.concatenate(halves(m), axis=0)


def split(x):
    hi = x.astype(BF16)
    return hi, (x - hi.astype(F32)).astype(BF16)


def mul_right(x, table):
    hi, lo = split(x)
    o = jnp.dot(jnp.concatenate([hi, lo], axis=1), table, preferred_element_type=F32)
    return o[:, :128] + o[:, 128:]


def mul_left(table, x):
    n = table.shape[0] // 2
    hi, lo = split(x)
    o = jnp.dot(table, hi, preferred_element_type=F32)
    return o[:n] + o[n:] + jnp.dot(table[:n], lo, preferred_element_type=F32)


def lanes_of(x, idx):
    return jnp.take_along_axis(x, jnp.broadcast_to(idx, x.shape), axis=1, mode="promise_in_bounds")


def rows_of(x, idx):
    return jnp.take_along_axis(x, idx, axis=0, mode="promise_in_bounds")


def lane(shape):
    return lax.broadcasted_iota(I32, shape, len(shape) - 1)


def sub(shape):
    return lax.broadcasted_iota(I32, shape, 0)


def pow2(e):
    n = e + 100
    r = jnp.full(e.shape, 2.0**-100, F32)
    for bit in range(7):
        r = r * jnp.where((n >> bit) & 1 == 1, 2.0 ** (1 << bit), 1.0)
    r = r * jnp.where((n >> 7) & 1 == 1, 2.0**64, 1.0)
    return r * jnp.where((n >> 7) & 1 == 1, 2.0**64, 1.0)


def exponent(top):
    e = jnp.floor(math.log2(32767.0) - jnp.log(jnp.maximum(top, 1e-35)) * (1 / math.log(2)))
    return jnp.clip(e, -60.0, 99.0).astype(I32)


def coded(x, e):
    v = jnp.floor(x * pow2(e) + 0.5)
    return jnp.clip(v, -32767.0, 32767.0).astype(I32).astype(I16)


def value(q, e):
    return q.astype(I32).astype(F32) * pow2(-e)


def term(hidden, grad, part):
    cols = 5120 // PARTS
    right = lax.slice_in_dim(grad, part * cols, (part + 1) * cols, axis=1)
    return lax.dot_general(hidden, right, (((0,), (0,)), ((), ())), preferred_element_type=F32)


def rows_for(hidden, core):
    yl = lax.axis_index("yl")
    own = lax.dynamic_slice_in_dim(hidden, 128 * (2 * yl + core), 128, axis=1)
    far = lax.dynamic_slice_in_dim(hidden, 128 * (2 * (1 - yl) + core), 128, axis=1)
    return jnp.concatenate([own, far], axis=1)


def place(group, pos):
    return pos if group == 0 else 5 + (pos + 1) % 5


def pick_tables():
    t = np.zeros((2, 8, 128), np.int32)
    for g in range(2):
        for ln in range(128):
            pos = min(ln // 16, 4) if ln < 80 else (ln - 80) % 5
            t[g, 0, ln] = place(g, pos)
            t[g, 1, ln] = 64 * (place(g, pos) % 2) if ln < 80 else 0
    return t


def code(x, q):
    for p in range(LEFT):
        exps = jnp.zeros((16, 128), I32)
        for t in range(5):
            at = GW * p + 128 * t
            v = x[:, at : at + 128]
            e = exponent(jnp.max(jnp.abs(v), axis=0, keepdims=True))
            q[p, 128 * t : 128 * t + 128, :] = coded(v, e)
            exps = jnp.where(sub((16, 128)) == t, jnp.broadcast_to(e, (16, 128)), exps)
        q[p, 640:656, :] = exps.astype(I16)


def code_kernel(own, got, q):
    code((own[...] + got[...]) * (1.0 / 64), q)


def code_alone(own, got):
    spec = pl.BlockSpec((128, LEFT * GW), lambda i: (1, i))
    return pl.pallas_call(
        code_kernel,
        grid=(PER // LEFT,),
        in_specs=[spec, spec],
        out_specs=pl.BlockSpec((LEFT, QROWS, 128), lambda i: (i, 0, 0)),
        out_shape=jax.ShapeDtypeStruct((PER, QROWS, 128), I16),
        compiler_params=ARB,
        cost_estimate=SHORT,
        name="code",
    )(own, got)


def compress_kernel(part, with_code, me, own, got, mom, picks, tab, rt, lt, *refs):
    pm, comp = refs[-2:]
    yl = me[0]
    first = 10 * (PER * part + LEFT * pl.program_id(0))
    ln = lane((1, 128))
    w0 = (own[:128] + got[:128]) * (1.0 / 64) + DECAY * mom[0]
    w1 = (own[128:] + got[128:]) * (1.0 / 64)
    pm[...] = w0
    if with_code:
        code(w1, refs[-3])
    tiles = []
    for t in range(5 * LEFT):
        tiles += [w0[:, 128 * t : 128 * t + 128], w1[:, 128 * t : 128 * t + 128]]
    o = mul_right(jnp.concatenate(tiles, axis=0), rt[...])
    tiles = [o[256 * t : 256 * t + 256] for t in range(5 * LEFT)]
    u16 = sub((16, 128))
    ln16 = lane((16, 128))
    short = []
    for k in range(2 * LEFT):
        g, at = k % 2, 5 * (k // 2)
        pieces = []
        span = first + 2 * at + tab[g, 0:1, :]
        for rb in range(4):
            qt = picks[rb // 2, rb % 2, 16:32, :]
            chosen = jnp.where(u16 == (ln16 & 15), lanes_of(qt, span), 0)
            idx = jnp.sum(chosen, axis=0, keepdims=True) + tab[g, 1:2, :]
            rows = slice(64 * rb, 64 * rb + 64)
            a = lanes_of(tiles[at + 3 * g][rows], idx)
            b = lanes_of(tiles[at + 3 * g + 1][rows], idx)
            c = lanes_of(tiles[at + 2][rows], idx)
            pieces.append(jnp.where(ln < 32, a, jnp.where(ln < 64, b, c)))
        short.append(jnp.concatenate(pieces, axis=0))
    z = mul_left(lt[...], jnp.concatenate(short, axis=1))
    for k in range(2 * LEFT):
        span = first + 10 * (k // 2) + tab[k % 2, 0:1, :]
        for rb in range(4):
            rel, a = rb // 2, rb % 2
            to = yl if rel == 0 else 1 - yl
            pt = picks[rel, a, 0:16, :]
            qt = picks[rel, a, 16:32, :]
            pidx, qidx = lanes_of(pt, span), lanes_of(qt, span)
            for h in range(2):
                pi = pidx[8 * h : 8 * h + 8]
                low, high = pi & 7, pi >> 3
                acc = jnp.where(ln < 85, pi, qidx[8 * h : 8 * h + 8]).astype(F32)
                for j in range(8):
                    r = 64 * rb + 8 * j
                    v = rows_of(z[r : r + 8, 128 * k : 128 * k + 128], low)
                    acc = jnp.where((high == j) & (ln < 80), v, acc)
                comp[a, k, to, 8 * h : 8 * h + 8, :] = acc


def compress(part, with_code, me, own, got, mom, picks, tab, rt, lt, before):
    n = PER // LEFT
    full = lambda *s: pl.BlockSpec(s, lambda i, me: (0,) * len(s))
    col = lambda r: pl.BlockSpec((r, LEFT * GW), lambda i, me: (0, i))
    args = [own, got, mom, picks, tab, rt, lt]
    in_specs = [
        col(256),
        col(256),
        pl.BlockSpec((1, 128, LEFT * GW), lambda i, me: (0, 0, part * n + i)),
        full(2, 2, 32, 128),
        full(2, 8, 128),
        full(256, 256),
        full(512, 256),
    ]
    alias = {}
    if before is not None:
        args.append(before)
        in_specs.append(pl.BlockSpec(memory_space=pl.ANY))
        alias = {8: 1 + with_code}
    return pl.pallas_call(
        functools.partial(compress_kernel, part, with_code),
        grid_spec=pltpu.PrefetchScalarGridSpec(
            num_scalar_prefetch=1,
            grid=(n,),
            in_specs=in_specs,
            out_specs=([pl.BlockSpec((LEFT, QROWS, 128), lambda i, me: (i, 0, 0))] if with_code else [])
            + [col(128), pl.BlockSpec((2, 2 * LEFT, 2, 16, 128), lambda i, me: (0, part * n + i, 0, 0, 0))],
        ),
        out_shape=([jax.ShapeDtypeStruct((PER, QROWS, 128), I16)] if with_code else [])
        + [
            jax.ShapeDtypeStruct((128, 5120 // PARTS), F32),
            jax.ShapeDtypeStruct((2, 16, 2, 16, 128), F32),
        ],
        input_output_aliases=alias,
        compiler_params=ARB,
        cost_estimate=SHORT,
        name="compress",
    )(me, *args)


def owner_kernel(got, rt, lt, out, xs, hot):
    ln16 = lane((16, 128))

    here = (ln16 & 63).astype(F32)
    u16 = sub((16, 128))

    def one(n, _):
        at = pl.multiple_of(16 * n, 16)
        x = got[2 * n]
        x = jnp.where(ln16 < 80, x + got[2 * n + 1], x)
        for t in range(3):
            half = 2 * t + (ln16 >> 6)
            hit = jnp.where(lanes_of(x, 85 + half) == here, 16 * half + u16 + 1, 0)
            if t == 2:
                hit = jnp.where(ln16 < 64, hit, 0)
            idx = jnp.broadcast_to(jnp.sum(hit, axis=0, keepdims=True), (16, 128)) - 1
            v = jnp.where(idx >= 0, lanes_of(x, jnp.maximum(idx, 0)), 0.0)
            hi, lo = split(v)
            xs[t, pl.ds(at, 16), :] = jnp.concatenate([hi, lo], axis=1)
            hot[t, pl.ds(at, 16), :] = jnp.where(lanes_of(x, 80 + half) == here, 1.0, 0.0).astype(BF16)
        return 0

    lax.fori_loop(0, got.shape[0] // 2, one, 0, unroll=8)
    same = (sub((128, 128)) >> 6) == (lane((128, 128)) >> 6)
    grids = []
    for t in range(3):
        d = lax.dot_general(hot[t], xs[t], (((0,), (0,)), ((), ())), preferred_element_type=F32)
        grids.append(jnp.where(same, d[:, :128] + d[:, 128:], 0.0))
    d = mul_right(jnp.concatenate(grids, axis=0), rt[...])
    u = mul_left(lt[...], jnp.concatenate([d[128 * t : 128 * t + 128] for t in range(3)], axis=1))
    u = u[:64] + u[64:]
    tiles = [u[:, 128 * t : 128 * t + 128] for t in range(3)]
    last = tiles[2]
    ln = lane((32, 128))
    tiles[2] = jnp.where(ln < 64, last[:32], jnp.roll(last[32:], 64, axis=1))
    x = jnp.concatenate(tiles, axis=0)
    e = exponent(jnp.max(jnp.abs(x), axis=0, keepdims=True))
    out[0:160, :] = coded(x, e)
    out[160:176, :] = jnp.broadcast_to(e, (16, 128)).astype(I16)


def owner(got, rt, lt):
    return pl.pallas_call(
        owner_kernel,
        out_shape=jax.ShapeDtypeStruct((UROWS, 128), I16),
        scratch_shapes=[pltpu.VMEM((3, 512, 256), BF16), pltpu.VMEM((3, 512, 128), BF16)],
        compiler_params=ARB,
        name="owner",
    )(got, rt, lt)


def decode(ref, pair):
    group = []
    for g in (2 * pair, 2 * pair + 1):
        e = ref[g, 160:176, :].astype(I32)[:1]
        group.append(value(ref[g, 0:160, :], e))
    even, odd = group
    lo = lane((32, 128)) < 64
    e2, o2 = even[128:160], odd[128:160]
    top = jnp.where(lo, e2, jnp.roll(o2, 64, axis=1))
    bottom = jnp.where(lo, jnp.roll(e2, 64, axis=1), o2)
    return [even[:64], even[64:128], jnp.concatenate([top, bottom], axis=0), odd[:64], odd[64:128]]


def finish_kernel(got0, got1, par, update, low, high):
    for a, (got, new) in enumerate(((got0, low), (got1, high))):
        rows = slice(64 * a, 64 * a + 64)
        for pair in range(LEFT):
            for t, u in enumerate(decode(got, pair)):
                cols = slice(GW * pair + 128 * t, GW * pair + 128 * t + 128)
                update[rows, cols] = u
                new[:, cols] = (par[rows, cols].astype(F32) - STEP * u).astype(BF16)


def finish(got, par):
    n = PAIRS // LEFT
    col = lambda r: pl.BlockSpec((r, LEFT * GW), lambda i: (0, i))
    blocks = lambda a: pl.BlockSpec((2 * LEFT, UROWS, 128), lambda i: (n * a + i, 0, 0))
    half = jax.ShapeDtypeStruct((64, 5120), BF16)
    return pl.pallas_call(
        finish_kernel,
        grid=(n,),
        in_specs=[blocks(0), blocks(1), col(128)],
        out_specs=[col(128), col(64), col(64)],
        out_shape=[jax.ShapeDtypeStruct((128, 5120), F32), half, half],
        compiler_params=ARB,
        cost_estimate=SHORT,
        name="finish",
    )(got, got, par)


def gather_kernel(n, rows, *refs):
    sem = refs[-1]
    out = refs[-2]
    copies = []
    for i in range(n):
        for k in range(4):
            at = pl.multiple_of(rows[i] + 16 * k, 16)
            copies.append(
                pltpu.make_async_copy(refs[i].at[16 * k : 16 * k + 16, :], out.at[pl.ds(at, 16), :], sem.at[4 * i + k])
            )
            copies[-1].start()
    for copy in copies:
        copy.wait()


def gather(rows, parts, before):
    n = len(parts)
    anywhere = pl.BlockSpec(memory_space=pl.ANY)
    args = list(parts) + ([] if before is None else [before])
    return pl.pallas_call(
        functools.partial(gather_kernel, n),
        grid_spec=pltpu.PrefetchScalarGridSpec(
            num_scalar_prefetch=1,
            grid=(1,),
            in_specs=[anywhere] * len(args),
            out_specs=anywhere,
            scratch_shapes=[pltpu.SemaphoreType.DMA((4 * n,))],
        ),
        out_shape=jax.ShapeDtypeStruct((512, 5120), BF16),
        input_output_aliases={} if before is None else {n + 1: 0},
        compiler_params=ARB,
        cost_estimate=pl.CostEstimate(flops=0, bytes_accessed=4 * 2**20, transcendentals=0),
        name="gather",
    )(rows, *args)


def left_kernel(part, q, pm, picks, rt, lt, irt, ilt, *refs):
    out, mask = refs[-2:]
    first = 10 * (PER * part + LEFT * pl.program_id(0))

    @pl.when(pl.program_id(0) == 0)
    def _():
        for a in range(2):
            k = sub((64, 128))
            hit = jnp.zeros((64, 128), F32)
            for u in range(16):
                hit = jnp.where(picks[0, a, u : u + 1, :] == k, 1.0, hit)
            mask[64 * a : 64 * a + 64, :] = hit

    ln16 = lane((16, 128))
    rows = sub((128, 128)) < 64
    moment, keep = [], []
    for t in range(5 * LEFT):
        e = q[t // 5, 640:656, :].astype(I32)[t % 5 : t % 5 + 1]
        at = 128 * (t % 5)
        moment.append(pm[:, 128 * t : 128 * t + 128] + value(q[t // 5, at : at + 128, :], e))
        span = first + 2 * t + (lane((1, 128)) >> 6)
        both = []
        for a in range(2):
            hit = lanes_of(picks[0, a, 16:32, :], span) == (ln16 & 63)
            both.append(jnp.max(jnp.where(hit, 1.0, 0.0), axis=0, keepdims=True))
        keep.append(lanes_of(mask[...], span) * jnp.where(rows, both[0], both[1]))
    n = len(moment)
    c = mul_right(jnp.concatenate(moment, axis=0), rt[...])
    c = mul_left(lt[...], jnp.concatenate([c[128 * t : 128 * t + 128] for t in range(n)], axis=1))
    c = mul_left(ilt[...], c * jnp.concatenate(keep, axis=1))
    r = mul_right(jnp.concatenate([c[:, 128 * t : 128 * t + 128] for t in range(n)], axis=0), irt[...])
    for t in range(n):
        out[0, :, 128 * t : 128 * t + 128] = moment[t] - r[128 * t : 128 * t + 128]


def left(part, q, pm, picks, rt, lt, irt, ilt, before):
    n = PER // LEFT
    full = lambda *s: pl.BlockSpec(s, lambda i: (0,) * len(s))
    args = [q, pm, picks, rt, lt, irt, ilt]
    in_specs = [
        pl.BlockSpec((LEFT, QROWS, 128), lambda i: (i, 0, 0)),
        pl.BlockSpec((128, LEFT * GW), lambda i: (0, i)),
        full(2, 2, 32, 128),
        full(256, 256),
        full(256, 128),
        full(256, 256),
        full(256, 128),
    ]
    alias = {}
    if before is not None:
        args.append(before)
        in_specs.append(pl.BlockSpec(memory_space=pl.ANY))
        alias = {7: 0}
    return pl.pallas_call(
        functools.partial(left_kernel, part),
        grid=(n,),
        in_specs=in_specs,
        out_specs=pl.BlockSpec((1, 128, LEFT * GW), lambda i: (0, 0, part * n + i)),
        out_shape=jax.ShapeDtypeStruct((1, 128, 5120), F32),
        scratch_shapes=[pltpu.VMEM((128, 128), F32)],
        input_output_aliases=alias,
        compiler_params=ARB,
        cost_estimate=SHORT,
        name="left",
    )(*args)


REP = ("x", "z", "yh")
NEAR = [(2 * h + k, 2 * h + 1 - k) for h in range(2) for k in range(2)]
FAR = [(y, 3 - y) for y in range(4)]
SWAP = [(0, 1), (1, 0)]


def body(hidden, grad, momentum, coef_picks, params):
    c = cosine()
    rt = jnp.asarray(right_table(diag(c.T, 2)))
    irt = jnp.asarray(right_table(diag(c, 2)))
    lt4 = jnp.asarray(left_table(diag(c, 4)))
    lt = jnp.asarray(left_table(diag(c, 2)))
    ilt = jnp.asarray(left_table(diag(c.T, 2)))
    tab = jnp.asarray(pick_tables())
    me = jnp.stack([lax.axis_index("yl"), lax.axis_index("c")]).astype(I32)

    mine = jnp.pad(coef_picks[0].swapaxes(1, 2), ((0, 0), (0, 0), (0, 48)))
    theirs = lax.ppermute(mine, ("yh", "yl"), NEAR)
    picks = jnp.stack([mine, theirs])

    core = lax.axis_index("c")
    sent = rows_for(hidden, 1 - core)
    kept = rows_for(hidden, core)
    swapped = [lax.ppermute(term(sent, grad, part), "c", SWAP) for part in range(PARTS)]
    own = [term(kept, grad, part) for part in range(PARTS)]
    tables = (momentum, picks, tab, rt, lt4)
    q0 = lax.ppermute(code_alone(own[0], swapped[0]), ("yh", "yl"), NEAR)
    pm0, comp = compress(0, False, me, own[0], swapped[0], *tables, None)
    q1, pm1, comp = compress(1, True, me, own[1], swapped[1], *tables, comp)
    q1 = lax.ppermute(q1, ("yh", "yl"), NEAR)
    comp, q0 = lax.optimization_barrier((comp, q0))
    got = lax.all_to_all(comp.reshape(64, 16, 128), REP + ("yl",), 0, 0, tiled=True)
    momentum_left = left(0, q0, pm0, picks, rt, lt, irt, ilt, None)
    got, momentum_left = lax.optimization_barrier((got, momentum_left))
    mine16 = owner(got, irt, ilt)
    mine16, q1 = lax.optimization_barrier((mine16, q1))
    every = lax.all_to_all(jnp.broadcast_to(mine16, (32, UROWS, 128)), REP, 0, 0, tiled=True)
    every, pm1 = lax.optimization_barrier((every, pm1))

    yl = lax.axis_index("yl")
    rows = lambda y, c: (128 * (2 * y + c) + 64 * jnp.arange(2)).astype(I32)
    update, low, high = finish(every, params)
    far_low = lax.ppermute(low, ("yh", "yl"), NEAR)
    far_high = lax.ppermute(high, ("yh", "yl"), FAR)
    momentum_left = left(1, q1, pm1, picks, rt, lt, irt, ilt, momentum_left)
    other = [lax.ppermute(v, "c", SWAP) for v in (low, high)]
    where = jnp.concatenate([rows(yl, core), rows(yl, 1 - core)])
    new = gather(where, [low, high, *other], None)
    far_low, far_high, new, momentum_left = lax.optimization_barrier((far_low, far_high, new, momentum_left))
    distant = [lax.ppermute(v, "c", SWAP) for v in (far_low, far_high)]
    new = gather(rows(1 - yl, core), [far_low, far_high], new)
    distant, new = lax.optimization_barrier((distant, new))
    new = gather(rows(1 - yl, 1 - core), distant, new)
    return momentum_left, update, new


def solution(mesh):
    fine = Mesh(mesh.devices.reshape(4, 4, 2, 2, 2), ("x", "z", "yh", "yl", "c"))
    rep, fsdp = ("x", "z", "yh"), ("yl", "c")
    return jax.shard_map(
        body,
        mesh=fine,
        in_specs=(
            P(rep + fsdp, None),
            P(rep + fsdp, None),
            P(rep, fsdp, None),
            P(rep, fsdp, None, None),
            P(fsdp, None),
        ),
        out_specs=(P(rep, fsdp, None), P(fsdp, None), P()),
        check_vma=False,
    )
```

```python
import functools
import math

import jax
import jax.numpy as jnp
import numpy as np
from jax import lax
from jax.experimental import pallas as pl
from jax.experimental.pallas import tpu as pltpu
from jax.sharding import Mesh
from jax.sharding import PartitionSpec as P

KEEP = 16
DECAY = 0.9
STEP = 0.5
PARTS = 2
PAIRS = 8
PER = PAIRS // PARTS
GW = 640
LEFT = 2
QROWS = 656
UROWS = 176
F32 = jnp.float32
BF16 = jnp.bfloat16
I16 = jnp.int16
I32 = jnp.int32
ARB = pltpu.CompilerParams(vmem_limit_bytes=20 * 1024 * 1024)


SHORT = pl.CostEstimate(flops=1000, bytes_accessed=1000, transcendentals=0)


def cosine():
    k = np.arange(64, dtype=np.float64)[:, None]
    i = np.arange(64, dtype=np.float64)[None, :]
    w = np.where(k == 0, math.sqrt(1.0 / 64), math.sqrt(2.0 / 64))
    return w * np.cos(math.pi * (2.0 * i + 1.0) * k / 128.0)


def halves(m):
    hi = m.astype(np.float32).astype(jnp.bfloat16)
    lo = (m - hi.astype(np.float64)).astype(np.float32).astype(jnp.bfloat16)
    return hi, lo


def diag(m, n):
    return np.kron(np.eye(n), m)


def right_table(m):
    hi, lo = halves(m)
    row = np.concatenate([hi, lo], axis=1)
    return np.concatenate([row, row], axis=0)


def left_table(m):
    return np.concatenate(halves(m), axis=0)


def split(x):
    hi = x.astype(BF16)
    return hi, (x - hi.astype(F32)).astype(BF16)


def mul_right(x, table):
    hi, lo = split(x)
    o = jnp.dot(jnp.concatenate([hi, lo], axis=1), table, preferred_element_type=F32)
    return o[:, :128] + o[:, 128:]


def mul_left(table, x):
    n = table.shape[0] // 2
    hi, lo = split(x)
    o = jnp.dot(table, hi, preferred_element_type=F32)
    return o[:n] + o[n:] + jnp.dot(table[:n], lo, preferred_element_type=F32)


def lanes_of(x, idx):
    return jnp.take_along_axis(x, jnp.broadcast_to(idx, x.shape), axis=1, mode="promise_in_bounds")


def rows_of(x, idx):
    return jnp.take_along_axis(x, idx, axis=0, mode="promise_in_bounds")


def lane(shape):
    return lax.broadcasted_iota(I32, shape, len(shape) - 1)


def sub(shape):
    return lax.broadcasted_iota(I32, shape, 0)


def pow2(e):
    n = e + 100
    r = jnp.full(e.shape, 2.0**-100, F32)
    for bit in range(7):
        r = r * jnp.where((n >> bit) & 1 == 1, 2.0 ** (1 << bit), 1.0)
    r = r * jnp.where((n >> 7) & 1 == 1, 2.0**64, 1.0)
    return r * jnp.where((n >> 7) & 1 == 1, 2.0**64, 1.0)


def exponent(top):
    e = jnp.floor(math.log2(32767.0) - jnp.log(jnp.maximum(top, 1e-35)) * (1 / math.log(2)))
    return jnp.clip(e, -60.0, 99.0).astype(I32)


def coded(x, e):
    v = jnp.floor(x * pow2(e) + 0.5)
    return jnp.clip(v, -32767.0, 32767.0).astype(I32).astype(I16)


def value(q, e):
    return q.astype(I32).astype(F32) * pow2(-e)


def term(hidden, grad, part):
    cols = 5120 // PARTS
    right = lax.slice_in_dim(grad, part * cols, (part + 1) * cols, axis=1)
    return lax.dot_general(hidden, right, (((0,), (0,)), ((), ())), preferred_element_type=F32)


def rows_for(hidden, core):
    yl = lax.axis_index("yl")
    own = lax.dynamic_slice_in_dim(hidden, 128 * (2 * yl + core), 128, axis=1)
    far = lax.dynamic_slice_in_dim(hidden, 128 * (2 * (1 - yl) + core), 128, axis=1)
    return jnp.concatenate([own, far], axis=1)


def place(group, pos):
    return pos if group == 0 else 5 + (pos + 1) % 5


def pick_tables():
    t = np.zeros((2, 8, 128), np.int32)
    for g in range(2):
        for ln in range(128):
            pos = min(ln // 16, 4) if ln < 80 else (ln - 80) % 5
            t[g, 0, ln] = place(g, pos)
            t[g, 1, ln] = 64 * (place(g, pos) % 2) if ln < 80 else 0
    return t


def code(x, q):
    for p in range(LEFT):
        exps = jnp.zeros((16, 128), I32)
        for t in range(5):
            at = GW * p + 128 * t
            v = x[:, at : at + 128]
            e = exponent(jnp.max(jnp.abs(v), axis=0, keepdims=True))
            q[p, 128 * t : 128 * t + 128, :] = coded(v, e)
            exps = jnp.where(sub((16, 128)) == t, jnp.broadcast_to(e, (16, 128)), exps)
        q[p, 640:656, :] = exps.astype(I16)


def code_kernel(own, got, q):
    code((own[...] + got[...]) * (1.0 / 64), q)


def code_alone(own, got):
    spec = pl.BlockSpec((128, LEFT * GW), lambda i: (1, i))
    return pl.pallas_call(
        code_kernel,
        grid=(PER // LEFT,),
        in_specs=[spec, spec],
        out_specs=pl.BlockSpec((LEFT, QROWS, 128), lambda i: (i, 0, 0)),
        out_shape=jax.ShapeDtypeStruct((PER, QROWS, 128), I16),
        compiler_params=ARB,
        cost_estimate=SHORT,
        name="code",
    )(own, got)


def compress_kernel(part, with_code, me, own, got, mom, picks, tab, rt, lt, *refs):
    pm, comp = refs[-2:]
    yl = me[0]
    first = 10 * (PER * part + LEFT * pl.program_id(0))
    ln = lane((1, 128))
    w0 = (own[:128] + got[:128]) * (1.0 / 64) + DECAY * mom[0]
    w1 = (own[128:] + got[128:]) * (1.0 / 64)
    pm[...] = w0
    if with_code:
        code(w1, refs[-3])
    tiles = []
    for t in range(5 * LEFT):
        tiles += [w0[:, 128 * t : 128 * t + 128], w1[:, 128 * t : 128 * t + 128]]
    o = mul_right(jnp.concatenate(tiles, axis=0), rt[...])
    tiles = [o[256 * t : 256 * t + 256] for t in range(5 * LEFT)]
    u16 = sub((16, 128))
    ln16 = lane((16, 128))
    short = []
    for k in range(2 * LEFT):
        g, at = k % 2, 5 * (k // 2)
        pieces = []
        span = first + 2 * at + tab[g, 0:1, :]
        for rb in range(4):
            qt = picks[rb // 2, rb % 2, 16:32, :]
            chosen = jnp.where(u16 == (ln16 & 15), lanes_of(qt, span), 0)
            idx = jnp.sum(chosen, axis=0, keepdims=True) + tab[g, 1:2, :]
            rows = slice(64 * rb, 64 * rb + 64)
            a = lanes_of(tiles[at + 3 * g][rows], idx)
            b = lanes_of(tiles[at + 3 * g + 1][rows], idx)
            c = lanes_of(tiles[at + 2][rows], idx)
            pieces.append(jnp.where(ln < 32, a, jnp.where(ln < 64, b, c)))
        short.append(jnp.concatenate(pieces, axis=0))
    z = mul_left(lt[...], jnp.concatenate(short, axis=1))
    for k in range(2 * LEFT):
        span = first + 10 * (k // 2) + tab[k % 2, 0:1, :]
        for rb in range(4):
            rel, a = rb // 2, rb % 2
            to = yl if rel == 0 else 1 - yl
            pt = picks[rel, a, 0:16, :]
            qt = picks[rel, a, 16:32, :]
            pidx, qidx = lanes_of(pt, span), lanes_of(qt, span)
            for h in range(2):
                pi = pidx[8 * h : 8 * h + 8]
                low, high = pi & 7, pi >> 3
                acc = jnp.where(ln < 85, pi, qidx[8 * h : 8 * h + 8]).astype(F32)
                for j in range(8):
                    r = 64 * rb + 8 * j
                    v = rows_of(z[r : r + 8, 128 * k : 128 * k + 128], low)
                    acc = jnp.where((high == j) & (ln < 80), v, acc)
                comp[a, k, to, 8 * h : 8 * h + 8, :] = acc


def compress(part, with_code, me, own, got, mom, picks, tab, rt, lt, before):
    n = PER // LEFT
    full = lambda *s: pl.BlockSpec(s, lambda i, me: (0,) * len(s))
    col = lambda r: pl.BlockSpec((r, LEFT * GW), lambda i, me: (0, i))
    args = [own, got, mom, picks, tab, rt, lt]
    in_specs = [
        col(256),
        col(256),
        pl.BlockSpec((1, 128, LEFT * GW), lambda i, me: (0, 0, part * n + i)),
        full(2, 2, 32, 128),
        full(2, 8, 128),
        full(256, 256),
        full(512, 256),
    ]
    alias = {}
    if before is not None:
        args.append(before)
        in_specs.append(pl.BlockSpec(memory_space=pl.ANY))
        alias = {8: 1 + with_code}
    return pl.pallas_call(
        functools.partial(compress_kernel, part, with_code),
        grid_spec=pltpu.PrefetchScalarGridSpec(
            num_scalar_prefetch=1,
            grid=(n,),
            in_specs=in_specs,
            out_specs=([pl.BlockSpec((LEFT, QROWS, 128), lambda i, me: (i, 0, 0))] if with_code else [])
            + [col(128), pl.BlockSpec((2, 2 * LEFT, 2, 16, 128), lambda i, me: (0, part * n + i, 0, 0, 0))],
        ),
        out_shape=([jax.ShapeDtypeStruct((PER, QROWS, 128), I16)] if with_code else [])
        + [
            jax.ShapeDtypeStruct((128, 5120 // PARTS), F32),
            jax.ShapeDtypeStruct((2, 16, 2, 16, 128), F32),
        ],
        input_output_aliases=alias,
        compiler_params=ARB,
        cost_estimate=SHORT,
        name="compress",
    )(me, *args)


def owner_kernel(got, rt, lt, out, xs, hot):
    ln16 = lane((16, 128))

    here = (ln16 & 63).astype(F32)
    u16 = sub((16, 128))

    def one(n, _):
        at = pl.multiple_of(16 * n, 16)
        x = got[2 * n]
        x = jnp.where(ln16 < 80, x + got[2 * n + 1], x)
        for t in range(3):
            half = 2 * t + (ln16 >> 6)
            hit = jnp.where(lanes_of(x, 85 + half) == here, 16 * half + u16 + 1, 0)
            if t == 2:
                hit = jnp.where(ln16 < 64, hit, 0)
            idx = jnp.broadcast_to(jnp.sum(hit, axis=0, keepdims=True), (16, 128)) - 1
            v = jnp.where(idx >= 0, lanes_of(x, jnp.maximum(idx, 0)), 0.0)
            hi, lo = split(v)
            xs[t, pl.ds(at, 16), :] = jnp.concatenate([hi, lo], axis=1)
            hot[t, pl.ds(at, 16), :] = jnp.where(lanes_of(x, 80 + half) == here, 1.0, 0.0).astype(BF16)
        return 0

    lax.fori_loop(0, got.shape[0] // 2, one, 0, unroll=4)
    same = (sub((128, 128)) >> 6) == (lane((128, 128)) >> 6)
    grids = []
    for t in range(3):
        d = lax.dot_general(hot[t], xs[t], (((0,), (0,)), ((), ())), preferred_element_type=F32)
        grids.append(jnp.where(same, d[:, :128] + d[:, 128:], 0.0))
    d = mul_right(jnp.concatenate(grids, axis=0), rt[...])
    u = mul_left(lt[...], jnp.concatenate([d[128 * t : 128 * t + 128] for t in range(3)], axis=1))
    u = u[:64] + u[64:]
    tiles = [u[:, 128 * t : 128 * t + 128] for t in range(3)]
    last = tiles[2]
    ln = lane((32, 128))
    tiles[2] = jnp.where(ln < 64, last[:32], jnp.roll(last[32:], 64, axis=1))
    x = jnp.concatenate(tiles, axis=0)
    e = exponent(jnp.max(jnp.abs(x), axis=0, keepdims=True))
    out[0:160, :] = coded(x, e)
    out[160:176, :] = jnp.broadcast_to(e, (16, 128)).astype(I16)


def owner(got, rt, lt):
    return pl.pallas_call(
        owner_kernel,
        out_shape=jax.ShapeDtypeStruct((UROWS, 128), I16),
        scratch_shapes=[pltpu.VMEM((3, 512, 256), BF16), pltpu.VMEM((3, 512, 128), BF16)],
        compiler_params=ARB,
        name="owner",
    )(got, rt, lt)


def decode(ref, pair):
    group = []
    for g in (2 * pair, 2 * pair + 1):
        e = ref[g, 160:176, :].astype(I32)[:1]
        group.append(value(ref[g, 0:160, :], e))
    even, odd = group
    lo = lane((32, 128)) < 64
    e2, o2 = even[128:160], odd[128:160]
    top = jnp.where(lo, e2, jnp.roll(o2, 64, axis=1))
    bottom = jnp.where(lo, jnp.roll(e2, 64, axis=1), o2)
    return [even[:64], even[64:128], jnp.concatenate([top, bottom], axis=0), odd[:64], odd[64:128]]


def finish_kernel(got0, got1, par, update, low, high):
    for a, (got, new) in enumerate(((got0, low), (got1, high))):
        rows = slice(64 * a, 64 * a + 64)
        for pair in range(LEFT):
            for t, u in enumerate(decode(got, pair)):
                cols = slice(GW * pair + 128 * t, GW * pair + 128 * t + 128)
                update[rows, cols] = u
                new[:, cols] = (par[rows, cols].astype(F32) - STEP * u).astype(BF16)


def finish(got, par):
    n = PAIRS // LEFT
    col = lambda r: pl.BlockSpec((r, LEFT * GW), lambda i: (0, i))
    blocks = lambda a: pl.BlockSpec((2 * LEFT, UROWS, 128), lambda i: (n * a + i, 0, 0))
    half = jax.ShapeDtypeStruct((64, 5120), BF16)
    return pl.pallas_call(
        finish_kernel,
        grid=(n,),
        in_specs=[blocks(0), blocks(1), col(128)],
        out_specs=[col(128), col(64), col(64)],
        out_shape=[jax.ShapeDtypeStruct((128, 5120), F32), half, half],
        compiler_params=ARB,
        cost_estimate=SHORT,
        name="finish",
    )(got, got, par)


def gather_kernel(n, rows, *refs):
    sem = refs[-1]
    out = refs[-2]
    copies = []
    for i in range(n):
        for k in range(4):
            at = pl.multiple_of(rows[i] + 16 * k, 16)
            copies.append(
                pltpu.make_async_copy(refs[i].at[16 * k : 16 * k + 16, :], out.at[pl.ds(at, 16), :], sem.at[4 * i + k])
            )
            copies[-1].start()
    for copy in copies:
        copy.wait()


def gather(rows, parts, before):
    n = len(parts)
    anywhere = pl.BlockSpec(memory_space=pl.ANY)
    args = list(parts) + ([] if before is None else [before])
    return pl.pallas_call(
        functools.partial(gather_kernel, n),
        grid_spec=pltpu.PrefetchScalarGridSpec(
            num_scalar_prefetch=1,
            grid=(1,),
            in_specs=[anywhere] * len(args),
            out_specs=anywhere,
            scratch_shapes=[pltpu.SemaphoreType.DMA((4 * n,))],
        ),
        out_shape=jax.ShapeDtypeStruct((512, 5120), BF16),
        input_output_aliases={} if before is None else {n + 1: 0},
        compiler_params=ARB,
        cost_estimate=pl.CostEstimate(flops=0, bytes_accessed=4 * 2**20, transcendentals=0),
        name="gather",
    )(rows, *args)


def left_kernel(part, q, pm, picks, rt, lt, irt, ilt, *refs):
    out, mask = refs[-2:]
    first = 10 * (PER * part + LEFT * pl.program_id(0))

    @pl.when(pl.program_id(0) == 0)
    def _():
        for a in range(2):
            k = sub((64, 128))
            hit = jnp.zeros((64, 128), F32)
            for u in range(16):
                hit = jnp.where(picks[0, a, u : u + 1, :] == k, 1.0, hit)
            mask[64 * a : 64 * a + 64, :] = hit

    ln16 = lane((16, 128))
    rows = sub((128, 128)) < 64
    moment, keep = [], []
    for t in range(5 * LEFT):
        e = q[t // 5, 640:656, :].astype(I32)[t % 5 : t % 5 + 1]
        at = 128 * (t % 5)
        moment.append(pm[:, 128 * t : 128 * t + 128] + value(q[t // 5, at : at + 128, :], e))
        span = first + 2 * t + (lane((1, 128)) >> 6)
        both = []
        for a in range(2):
            hit = lanes_of(picks[0, a, 16:32, :], span) == (ln16 & 63)
            both.append(jnp.max(jnp.where(hit, 1.0, 0.0), axis=0, keepdims=True))
        keep.append(lanes_of(mask[...], span) * jnp.where(rows, both[0], both[1]))
    n = len(moment)
    c = mul_right(jnp.concatenate(moment, axis=0), rt[...])
    c = mul_left(lt[...], jnp.concatenate([c[128 * t : 128 * t + 128] for t in range(n)], axis=1))
    c = mul_left(ilt[...], c * jnp.concatenate(keep, axis=1))
    r = mul_right(jnp.concatenate([c[:, 128 * t : 128 * t + 128] for t in range(n)], axis=0), irt[...])
    for t in range(n):
        out[0, :, 128 * t : 128 * t + 128] = moment[t] - r[128 * t : 128 * t + 128]


def left(part, q, pm, picks, rt, lt, irt, ilt, before):
    n = PER // LEFT
    full = lambda *s: pl.BlockSpec(s, lambda i: (0,) * len(s))
    args = [q, pm, picks, rt, lt, irt, ilt]
    in_specs = [
        pl.BlockSpec((LEFT, QROWS, 128), lambda i: (i, 0, 0)),
        pl.BlockSpec((128, LEFT * GW), lambda i: (0, i)),
        full(2, 2, 32, 128),
        full(256, 256),
        full(256, 128),
        full(256, 256),
        full(256, 128),
    ]
    alias = {}
    if before is not None:
        args.append(before)
        in_specs.append(pl.BlockSpec(memory_space=pl.ANY))
        alias = {7: 0}
    return pl.pallas_call(
        functools.partial(left_kernel, part),
        grid=(n,),
        in_specs=in_specs,
        out_specs=pl.BlockSpec((1, 128, LEFT * GW), lambda i: (0, 0, part * n + i)),
        out_shape=jax.ShapeDtypeStruct((1, 128, 5120), F32),
        scratch_shapes=[pltpu.VMEM((128, 128), F32)],
        input_output_aliases=alias,
        compiler_params=ARB,
        cost_estimate=SHORT,
        name="left",
    )(*args)


REP = ("x", "z", "yh")
NEAR = [(2 * h + k, 2 * h + 1 - k) for h in range(2) for k in range(2)]
FAR = [(y, 3 - y) for y in range(4)]
SWAP = [(0, 1), (1, 0)]


def body(hidden, grad, momentum, coef_picks, params):
    c = cosine()
    rt = jnp.asarray(right_table(diag(c.T, 2)))
    irt = jnp.asarray(right_table(diag(c, 2)))
    lt4 = jnp.asarray(left_table(diag(c, 4)))
    lt = jnp.asarray(left_table(diag(c, 2)))
    ilt = jnp.asarray(left_table(diag(c.T, 2)))
    tab = jnp.asarray(pick_tables())
    me = jnp.stack([lax.axis_index("yl"), lax.axis_index("c")]).astype(I32)

    mine = jnp.pad(coef_picks[0].swapaxes(1, 2), ((0, 0), (0, 0), (0, 48)))
    theirs = lax.ppermute(mine, ("yh", "yl"), NEAR)
    picks = jnp.stack([mine, theirs])

    core = lax.axis_index("c")
    sent = rows_for(hidden, 1 - core)
    kept = rows_for(hidden, core)
    swapped = [lax.ppermute(term(sent, grad, part), "c", SWAP) for part in range(PARTS)]
    own = [term(kept, grad, part) for part in range(PARTS)]
    tables = (momentum, picks, tab, rt, lt4)
    q0 = lax.ppermute(code_alone(own[0], swapped[0]), ("yh", "yl"), NEAR)
    pm0, comp = compress(0, False, me, own[0], swapped[0], *tables, None)
    q1, pm1, comp = compress(1, True, me, own[1], swapped[1], *tables, comp)
    q1 = lax.ppermute(q1, ("yh", "yl"), NEAR)
    comp, q0 = lax.optimization_barrier((comp, q0))
    got = lax.all_to_all(comp.reshape(64, 16, 128), REP + ("yl",), 0, 0, tiled=True)
    momentum_left = left(0, q0, pm0, picks, rt, lt, irt, ilt, None)
    got, momentum_left = lax.optimization_barrier((got, momentum_left))
    mine16 = owner(got, irt, ilt)
    mine16, q1 = lax.optimization_barrier((mine16, q1))
    every = lax.all_to_all(jnp.broadcast_to(mine16, (32, UROWS, 128)), REP, 0, 0, tiled=True)
    every, pm1 = lax.optimization_barrier((every, pm1))

    yl = lax.axis_index("yl")
    rows = lambda y, c: (128 * (2 * y + c) + 64 * jnp.arange(2)).astype(I32)
    update, low, high = finish(every, params)
    far_low = lax.ppermute(low, ("yh", "yl"), NEAR)
    far_high = lax.ppermute(high, ("yh", "yl"), FAR)
    momentum_left = left(1, q1, pm1, picks, rt, lt, irt, ilt, momentum_left)
    other = [lax.ppermute(v, "c", SWAP) for v in (low, high)]
    where = jnp.concatenate([rows(yl, core), rows(yl, 1 - core)])
    new = gather(where, [low, high, *other], None)
    far_low, far_high, new, momentum_left = lax.optimization_barrier((far_low, far_high, new, momentum_left))
    distant = [lax.ppermute(v, "c", SWAP) for v in (far_low, far_high)]
    new = gather(rows(1 - yl, core), [far_low, far_high], new)
    distant, new = lax.optimization_barrier((distant, new))
    new = gather(rows(1 - yl, 1 - core), distant, new)
    return momentum_left, update, new


def solution(mesh):
    fine = Mesh(mesh.devices.reshape(4, 4, 2, 2, 2), ("x", "z", "yh", "yl", "c"))
    rep, fsdp = ("x", "z", "yh"), ("yl", "c")
    return jax.shard_map(
        body,
        mesh=fine,
        in_specs=(
            P(rep + fsdp, None),
            P(rep + fsdp, None),
            P(rep, fsdp, None),
            P(rep, fsdp, None, None),
            P(fsdp, None),
        ),
        out_specs=(P(rep, fsdp, None), P(fsdp, None), P()),
        check_vma=False,
    )
```

```python
import functools
import math

import jax
import jax.numpy as jnp
import numpy as np
from jax import lax
from jax.experimental import pallas as pl
from jax.experimental.pallas import tpu as pltpu
from jax.sharding import Mesh
from jax.sharding import PartitionSpec as P

KEEP = 16
DECAY = 0.9
STEP = 0.5
PARTS = 2
PAIRS = 8
PER = PAIRS // PARTS
GW = 640
FINISH = 4
LEFT = 2
QROWS = 656
UROWS = 176
F32 = jnp.float32
BF16 = jnp.bfloat16
I16 = jnp.int16
I32 = jnp.int32
ARB = pltpu.CompilerParams(vmem_limit_bytes=20 * 1024 * 1024)


SHORT = pl.CostEstimate(flops=1000, bytes_accessed=1000, transcendentals=0)


def cosine():
    k = np.arange(64, dtype=np.float64)[:, None]
    i = np.arange(64, dtype=np.float64)[None, :]
    w = np.where(k == 0, math.sqrt(1.0 / 64), math.sqrt(2.0 / 64))
    return w * np.cos(math.pi * (2.0 * i + 1.0) * k / 128.0)


def halves(m):
    hi = m.astype(np.float32).astype(jnp.bfloat16)
    lo = (m - hi.astype(np.float64)).astype(np.float32).astype(jnp.bfloat16)
    return hi, lo


def diag(m, n):
    return np.kron(np.eye(n), m)


def right_table(m):
    hi, lo = halves(m)
    row = np.concatenate([hi, lo], axis=1)
    return np.concatenate([row, row], axis=0)


def left_table(m):
    return np.concatenate(halves(m), axis=0)


def split(x):
    hi = x.astype(BF16)
    return hi, (x - hi.astype(F32)).astype(BF16)


def mul_right(x, table):
    hi, lo = split(x)
    o = jnp.dot(jnp.concatenate([hi, lo], axis=1), table, preferred_element_type=F32)
    return o[:, :128] + o[:, 128:]


def mul_left(table, x):
    n = table.shape[0] // 2
    hi, lo = split(x)
    o = jnp.dot(table, hi, preferred_element_type=F32)
    return o[:n] + o[n:] + jnp.dot(table[:n], lo, preferred_element_type=F32)


def lanes_of(x, idx):
    return jnp.take_along_axis(x, jnp.broadcast_to(idx, x.shape), axis=1, mode="promise_in_bounds")


def rows_of(x, idx):
    return jnp.take_along_axis(x, idx, axis=0, mode="promise_in_bounds")


def lane(shape):
    return lax.broadcasted_iota(I32, shape, len(shape) - 1)


def sub(shape):
    return lax.broadcasted_iota(I32, shape, 0)


def pow2(e):
    n = e + 100
    r = jnp.full(e.shape, 2.0**-100, F32)
    for bit in range(7):
        r = r * jnp.where((n >> bit) & 1 == 1, 2.0 ** (1 << bit), 1.0)
    r = r * jnp.where((n >> 7) & 1 == 1, 2.0**64, 1.0)
    return r * jnp.where((n >> 7) & 1 == 1, 2.0**64, 1.0)


def exponent(top):
    e = jnp.floor(math.log2(32767.0) - jnp.log(jnp.maximum(top, 1e-35)) * (1 / math.log(2)))
    return jnp.clip(e, -60.0, 99.0).astype(I32)


def coded(x, e):
    v = jnp.floor(x * pow2(e) + 0.5)
    return jnp.clip(v, -32767.0, 32767.0).astype(I32).astype(I16)


def value(q, e):
    return q.astype(I32).astype(F32) * pow2(-e)


def term(hidden, grad, part):
    cols = 5120 // PARTS
    right = lax.slice_in_dim(grad, part * cols, (part + 1) * cols, axis=1)
    return lax.dot_general(hidden, right, (((0,), (0,)), ((), ())), preferred_element_type=F32)


def rows_for(hidden, core):
    yl = lax.axis_index("yl")
    own = lax.dynamic_slice_in_dim(hidden, 128 * (2 * yl + core), 128, axis=1)
    far = lax.dynamic_slice_in_dim(hidden, 128 * (2 * (1 - yl) + core), 128, axis=1)
    return jnp.concatenate([own, far], axis=1)


def place(group, pos):
    return pos if group == 0 else 5 + (pos + 1) % 5


def pick_tables():
    t = np.zeros((2, 8, 128), np.int32)
    for g in range(2):
        for ln in range(128):
            pos = min(ln // 16, 4) if ln < 80 else (ln - 80) % 5
            t[g, 0, ln] = place(g, pos)
            t[g, 1, ln] = 64 * (place(g, pos) % 2) if ln < 80 else 0
    return t


def code(x, q):
    for p in range(LEFT):
        exps = jnp.zeros((16, 128), I32)
        for t in range(5):
            at = GW * p + 128 * t
            v = x[:, at : at + 128]
            e = exponent(jnp.max(jnp.abs(v), axis=0, keepdims=True))
            q[p, 128 * t : 128 * t + 128, :] = coded(v, e)
            exps = jnp.where(sub((16, 128)) == t, jnp.broadcast_to(e, (16, 128)), exps)
        q[p, 640:656, :] = exps.astype(I16)


def code_kernel(own, got, q):
    code((own[...] + got[...]) * (1.0 / 64), q)


def code_alone(own, got):
    spec = pl.BlockSpec((128, LEFT * GW), lambda i: (1, i))
    return pl.pallas_call(
        code_kernel,
        grid=(PER // LEFT,),
        in_specs=[spec, spec],
        out_specs=pl.BlockSpec((LEFT, QROWS, 128), lambda i: (i, 0, 0)),
        out_shape=jax.ShapeDtypeStruct((PER, QROWS, 128), I16),
        compiler_params=ARB,
        cost_estimate=SHORT,
        name="code",
    )(own, got)


def compress_kernel(part, with_code, me, own, got, mom, picks, tab, rt, lt, *refs):
    pm, comp = refs[-2:]
    yl = me[0]
    first = 10 * (PER * part + LEFT * pl.program_id(0))
    ln = lane((1, 128))
    w0 = (own[:128] + got[:128]) * (1.0 / 64) + DECAY * mom[0]
    w1 = (own[128:] + got[128:]) * (1.0 / 64)
    pm[...] = w0
    if with_code:
        code(w1, refs[-3])
    tiles = []
    for t in range(5 * LEFT):
        tiles += [w0[:, 128 * t : 128 * t + 128], w1[:, 128 * t : 128 * t + 128]]
    o = mul_right(jnp.concatenate(tiles, axis=0), rt[...])
    tiles = [o[256 * t : 256 * t + 256] for t in range(5 * LEFT)]
    u16 = sub((16, 128))
    ln16 = lane((16, 128))
    short = []
    for k in range(2 * LEFT):
        g, at = k % 2, 5 * (k // 2)
        pieces = []
        span = first + 2 * at + tab[g, 0:1, :]
        for rb in range(4):
            qt = picks[rb // 2, rb % 2, 16:32, :]
            chosen = jnp.where(u16 == (ln16 & 15), lanes_of(qt, span), 0)
            idx = jnp.sum(chosen, axis=0, keepdims=True) + tab[g, 1:2, :]
            rows = slice(64 * rb, 64 * rb + 64)
            a = lanes_of(tiles[at + 3 * g][rows], idx)
            b = lanes_of(tiles[at + 3 * g + 1][rows], idx)
            c = lanes_of(tiles[at + 2][rows], idx)
            pieces.append(jnp.where(ln < 32, a, jnp.where(ln < 64, b, c)))
        short.append(jnp.concatenate(pieces, axis=0))
    z = mul_left(lt[...], jnp.concatenate(short, axis=1))
    for k in range(2 * LEFT):
        span = first + 10 * (k // 2) + tab[k % 2, 0:1, :]
        for rb in range(4):
            rel, a = rb // 2, rb % 2
            to = yl if rel == 0 else 1 - yl
            pt = picks[rel, a, 0:16, :]
            qt = picks[rel, a, 16:32, :]
            pidx, qidx = lanes_of(pt, span), lanes_of(qt, span)
            for h in range(2):
                pi = pidx[8 * h : 8 * h + 8]
                low, high = pi & 7, pi >> 3
                acc = jnp.where(ln < 85, pi, qidx[8 * h : 8 * h + 8]).astype(F32)
                for j in range(8):
                    r = 64 * rb + 8 * j
                    v = rows_of(z[r : r + 8, 128 * k : 128 * k + 128], low)
                    acc = jnp.where((high == j) & (ln < 80), v, acc)
                comp[a, k, to, 8 * h : 8 * h + 8, :] = acc


def compress(part, with_code, me, own, got, mom, picks, tab, rt, lt, before):
    n = PER // LEFT
    full = lambda *s: pl.BlockSpec(s, lambda i, me: (0,) * len(s))
    col = lambda r: pl.BlockSpec((r, LEFT * GW), lambda i, me: (0, i))
    args = [own, got, mom, picks, tab, rt, lt]
    in_specs = [
        col(256),
        col(256),
        pl.BlockSpec((1, 128, LEFT * GW), lambda i, me: (0, 0, part * n + i)),
        full(2, 2, 32, 128),
        full(2, 8, 128),
        full(256, 256),
        full(512, 256),
    ]
    alias = {}
    if before is not None:
        args.append(before)
        in_specs.append(pl.BlockSpec(memory_space=pl.ANY))
        alias = {8: 1 + with_code}
    return pl.pallas_call(
        functools.partial(compress_kernel, part, with_code),
        grid_spec=pltpu.PrefetchScalarGridSpec(
            num_scalar_prefetch=1,
            grid=(n,),
            in_specs=in_specs,
            out_specs=([pl.BlockSpec((LEFT, QROWS, 128), lambda i, me: (i, 0, 0))] if with_code else [])
            + [col(128), pl.BlockSpec((2, 2 * LEFT, 2, 16, 128), lambda i, me: (0, part * n + i, 0, 0, 0))],
        ),
        out_shape=([jax.ShapeDtypeStruct((PER, QROWS, 128), I16)] if with_code else [])
        + [
            jax.ShapeDtypeStruct((128, 5120 // PARTS), F32),
            jax.ShapeDtypeStruct((2, 16, 2, 16, 128), F32),
        ],
        input_output_aliases=alias,
        compiler_params=ARB,
        cost_estimate=SHORT,
        name="compress",
    )(me, *args)


def owner_kernel(got, rt, lt, out, xs, hot):
    ln16 = lane((16, 128))

    here = (ln16 & 63).astype(F32)
    u16 = sub((16, 128))

    def one(n, _):
        at = pl.multiple_of(16 * n, 16)
        x = got[2 * n]
        x = jnp.where(ln16 < 80, x + got[2 * n + 1], x)
        for t in range(3):
            half = 2 * t + (ln16 >> 6)
            hit = jnp.where(lanes_of(x, 85 + half) == here, 16 * half + u16 + 1, 0)
            if t == 2:
                hit = jnp.where(ln16 < 64, hit, 0)
            idx = jnp.broadcast_to(jnp.sum(hit, axis=0, keepdims=True), (16, 128)) - 1
            v = jnp.where(idx >= 0, lanes_of(x, jnp.maximum(idx, 0)), 0.0)
            hi, lo = split(v)
            xs[t, pl.ds(at, 16), :] = jnp.concatenate([hi, lo], axis=1)
            hot[t, pl.ds(at, 16), :] = jnp.where(lanes_of(x, 80 + half) == here, 1.0, 0.0).astype(BF16)
        return 0

    lax.fori_loop(0, got.shape[0] // 2, one, 0, unroll=4)
    same = (sub((128, 128)) >> 6) == (lane((128, 128)) >> 6)
    grids = []
    for t in range(3):
        d = lax.dot_general(hot[t], xs[t], (((0,), (0,)), ((), ())), preferred_element_type=F32)
        grids.append(jnp.where(same, d[:, :128] + d[:, 128:], 0.0))
    d = mul_right(jnp.concatenate(grids, axis=0), rt[...])
    u = mul_left(lt[...], jnp.concatenate([d[128 * t : 128 * t + 128] for t in range(3)], axis=1))
    u = u[:64] + u[64:]
    tiles = [u[:, 128 * t : 128 * t + 128] for t in range(3)]
    last = tiles[2]
    ln = lane((32, 128))
    tiles[2] = jnp.where(ln < 64, last[:32], jnp.roll(last[32:], 64, axis=1))
    x = jnp.concatenate(tiles, axis=0)
    e = exponent(jnp.max(jnp.abs(x), axis=0, keepdims=True))
    out[0:160, :] = coded(x, e)
    out[160:176, :] = jnp.broadcast_to(e, (16, 128)).astype(I16)


def owner(got, rt, lt):
    return pl.pallas_call(
        owner_kernel,
        out_shape=jax.ShapeDtypeStruct((UROWS, 128), I16),
        scratch_shapes=[pltpu.VMEM((3, 512, 256), BF16), pltpu.VMEM((3, 512, 128), BF16)],
        compiler_params=ARB,
        name="owner",
    )(got, rt, lt)


def decode(ref, pair):
    group = []
    for g in (2 * pair, 2 * pair + 1):
        e = ref[g, 160:176, :].astype(I32)[:1]
        group.append(value(ref[g, 0:160, :], e))
    even, odd = group
    lo = lane((32, 128)) < 64
    e2, o2 = even[128:160], odd[128:160]
    top = jnp.where(lo, e2, jnp.roll(o2, 64, axis=1))
    bottom = jnp.where(lo, jnp.roll(e2, 64, axis=1), o2)
    return [even[:64], even[64:128], jnp.concatenate([top, bottom], axis=0), odd[:64], odd[64:128]]


def finish_kernel(got0, got1, par, update, low, high):
    for a, (got, new) in enumerate(((got0, low), (got1, high))):
        rows = slice(64 * a, 64 * a + 64)
        for pair in range(FINISH):
            for t, u in enumerate(decode(got, pair)):
                cols = slice(GW * pair + 128 * t, GW * pair + 128 * t + 128)
                update[rows, cols] = u
                new[:, cols] = (par[rows, cols].astype(F32) - STEP * u).astype(BF16)


def finish(got, par):
    n = PAIRS // FINISH
    col = lambda r: pl.BlockSpec((r, FINISH * GW), lambda i: (0, i))
    blocks = lambda a: pl.BlockSpec((2 * FINISH, UROWS, 128), lambda i: (n * a + i, 0, 0))
    half = jax.ShapeDtypeStruct((64, 5120), BF16)
    return pl.pallas_call(
        finish_kernel,
        grid=(n,),
        in_specs=[blocks(0), blocks(1), col(128)],
        out_specs=[col(128), col(64), col(64)],
        out_shape=[jax.ShapeDtypeStruct((128, 5120), F32), half, half],
        compiler_params=ARB,
        cost_estimate=SHORT,
        name="finish",
    )(got, got, par)


def gather_kernel(n, rows, *refs):
    sem = refs[-1]
    out = refs[-2]
    copies = []
    for i in range(n):
        for k in range(4):
            at = pl.multiple_of(rows[i] + 16 * k, 16)
            copies.append(
                pltpu.make_async_copy(refs[i].at[16 * k : 16 * k + 16, :], out.at[pl.ds(at, 16), :], sem.at[4 * i + k])
            )
            copies[-1].start()
    for copy in copies:
        copy.wait()


def gather(rows, parts, before):
    n = len(parts)
    anywhere = pl.BlockSpec(memory_space=pl.ANY)
    args = list(parts) + ([] if before is None else [before])
    return pl.pallas_call(
        functools.partial(gather_kernel, n),
        grid_spec=pltpu.PrefetchScalarGridSpec(
            num_scalar_prefetch=1,
            grid=(1,),
            in_specs=[anywhere] * len(args),
            out_specs=anywhere,
            scratch_shapes=[pltpu.SemaphoreType.DMA((4 * n,))],
        ),
        out_shape=jax.ShapeDtypeStruct((512, 5120), BF16),
        input_output_aliases={} if before is None else {n + 1: 0},
        compiler_params=ARB,
        cost_estimate=pl.CostEstimate(flops=0, bytes_accessed=4 * 2**20, transcendentals=0),
        name="gather",
    )(rows, *args)


def left_kernel(part, q, pm, picks, rt, lt, irt, ilt, *refs):
    out, mask = refs[-2:]
    first = 10 * (PER * part + LEFT * pl.program_id(0))

    @pl.when(pl.program_id(0) == 0)
    def _():
        for a in range(2):
            k = sub((64, 128))
            hit = jnp.zeros((64, 128), F32)
            for u in range(16):
                hit = jnp.where(picks[0, a, u : u + 1, :] == k, 1.0, hit)
            mask[64 * a : 64 * a + 64, :] = hit

    ln16 = lane((16, 128))
    rows = sub((128, 128)) < 64
    moment, keep = [], []
    for t in range(5 * LEFT):
        e = q[t // 5, 640:656, :].astype(I32)[t % 5 : t % 5 + 1]
        at = 128 * (t % 5)
        moment.append(pm[:, 128 * t : 128 * t + 128] + value(q[t // 5, at : at + 128, :], e))
        span = first + 2 * t + (lane((1, 128)) >> 6)
        both = []
        for a in range(2):
            hit = lanes_of(picks[0, a, 16:32, :], span) == (ln16 & 63)
            both.append(jnp.max(jnp.where(hit, 1.0, 0.0), axis=0, keepdims=True))
        keep.append(lanes_of(mask[...], span) * jnp.where(rows, both[0], both[1]))
    n = len(moment)
    c = mul_right(jnp.concatenate(moment, axis=0), rt[...])
    c = mul_left(lt[...], jnp.concatenate([c[128 * t : 128 * t + 128] for t in range(n)], axis=1))
    c = mul_left(ilt[...], c * jnp.concatenate(keep, axis=1))
    r = mul_right(jnp.concatenate([c[:, 128 * t : 128 * t + 128] for t in range(n)], axis=0), irt[...])
    for t in range(n):
        out[0, :, 128 * t : 128 * t + 128] = moment[t] - r[128 * t : 128 * t + 128]


def left(part, q, pm, picks, rt, lt, irt, ilt, before):
    n = PER // LEFT
    full = lambda *s: pl.BlockSpec(s, lambda i: (0,) * len(s))
    args = [q, pm, picks, rt, lt, irt, ilt]
    in_specs = [
        pl.BlockSpec((LEFT, QROWS, 128), lambda i: (i, 0, 0)),
        pl.BlockSpec((128, LEFT * GW), lambda i: (0, i)),
        full(2, 2, 32, 128),
        full(256, 256),
        full(256, 128),
        full(256, 256),
        full(256, 128),
    ]
    alias = {}
    if before is not None:
        args.append(before)
        in_specs.append(pl.BlockSpec(memory_space=pl.ANY))
        alias = {7: 0}
    return pl.pallas_call(
        functools.partial(left_kernel, part),
        grid=(n,),
        in_specs=in_specs,
        out_specs=pl.BlockSpec((1, 128, LEFT * GW), lambda i: (0, 0, part * n + i)),
        out_shape=jax.ShapeDtypeStruct((1, 128, 5120), F32),
        scratch_shapes=[pltpu.VMEM((128, 128), F32)],
        input_output_aliases=alias,
        compiler_params=ARB,
        cost_estimate=SHORT,
        name="left",
    )(*args)


REP = ("x", "z", "yh")
NEAR = [(2 * h + k, 2 * h + 1 - k) for h in range(2) for k in range(2)]
FAR = [(y, 3 - y) for y in range(4)]
SWAP = [(0, 1), (1, 0)]


def body(hidden, grad, momentum, coef_picks, params):
    c = cosine()
    rt = jnp.asarray(right_table(diag(c.T, 2)))
    irt = jnp.asarray(right_table(diag(c, 2)))
    lt4 = jnp.asarray(left_table(diag(c, 4)))
    lt = jnp.asarray(left_table(diag(c, 2)))
    ilt = jnp.asarray(left_table(diag(c.T, 2)))
    tab = jnp.asarray(pick_tables())
    me = jnp.stack([lax.axis_index("yl"), lax.axis_index("c")]).astype(I32)

    mine = jnp.pad(coef_picks[0].swapaxes(1, 2), ((0, 0), (0, 0), (0, 48)))
    theirs = lax.ppermute(mine, ("yh", "yl"), NEAR)
    picks = jnp.stack([mine, theirs])

    core = lax.axis_index("c")
    sent = rows_for(hidden, 1 - core)
    kept = rows_for(hidden, core)
    swapped = [lax.ppermute(term(sent, grad, part), "c", SWAP) for part in range(PARTS)]
    own = [term(kept, grad, part) for part in range(PARTS)]
    tables = (momentum, picks, tab, rt, lt4)
    q0 = lax.ppermute(code_alone(own[0], swapped[0]), ("yh", "yl"), NEAR)
    pm0, comp = compress(0, False, me, own[0], swapped[0], *tables, None)
    q1, pm1, comp = compress(1, True, me, own[1], swapped[1], *tables, comp)
    q1 = lax.ppermute(q1, ("yh", "yl"), NEAR)
    comp, q0 = lax.optimization_barrier((comp, q0))
    got = lax.all_to_all(comp.reshape(64, 16, 128), REP + ("yl",), 0, 0, tiled=True)
    momentum_left = left(0, q0, pm0, picks, rt, lt, irt, ilt, None)
    got, momentum_left = lax.optimization_barrier((got, momentum_left))
    mine16 = owner(got, irt, ilt)
    mine16, q1 = lax.optimization_barrier((mine16, q1))
    every = lax.all_to_all(jnp.broadcast_to(mine16, (32, UROWS, 128)), REP, 0, 0, tiled=True)
    every, pm1 = lax.optimization_barrier((every, pm1))

    yl = lax.axis_index("yl")
    rows = lambda y, c: (128 * (2 * y + c) + 64 * jnp.arange(2)).astype(I32)
    update, low, high = finish(every, params)
    far_low = lax.ppermute(low, ("yh", "yl"), NEAR)
    far_high = lax.ppermute(high, ("yh", "yl"), FAR)
    momentum_left = left(1, q1, pm1, picks, rt, lt, irt, ilt, momentum_left)
    other = [lax.ppermute(v, "c", SWAP) for v in (low, high)]
    where = jnp.concatenate([rows(yl, core), rows(yl, 1 - core)])
    new = gather(where, [low, high, *other], None)
    far_low, far_high, new, momentum_left = lax.optimization_barrier((far_low, far_high, new, momentum_left))
    distant = [lax.ppermute(v, "c", SWAP) for v in (far_low, far_high)]
    new = gather(rows(1 - yl, core), [far_low, far_high], new)
    distant, new = lax.optimization_barrier((distant, new))
    new = gather(rows(1 - yl, 1 - core), distant, new)
    return momentum_left, update, new


def solution(mesh):
    fine = Mesh(mesh.devices.reshape(4, 4, 2, 2, 2), ("x", "z", "yh", "yl", "c"))
    rep, fsdp = ("x", "z", "yh"), ("yl", "c")
    return jax.shard_map(
        body,
        mesh=fine,
        in_specs=(
            P(rep + fsdp, None),
            P(rep + fsdp, None),
            P(rep, fsdp, None),
            P(rep, fsdp, None, None),
            P(fsdp, None),
        ),
        out_specs=(P(rep, fsdp, None), P(fsdp, None), P()),
        check_vma=False,
    )
```
